128 devices in a mesh: lat: 8 (over y, core), lon: 16 (over x, z).
Axes of the slice: x: 4, y: 4, z: 4, core: 2. Of those that a mesh axis runs over, the one named last changes fastest.
Arguments:
- spectra: float32 [1800, 128, 1024], P(None, 'lon', 'lat'), may hold values from 0 to 2.1, as said below
- sea_mask: int32 [128, 1024], P('lon', 'lat'), may hold values 0 or 1
- atm_wind: float32 [2, 262144], P(None, ('lat', 'lon')), may hold values from -10 to 10
- wind_row: int32 [128, 1024], P('lon', 'lat'), may hold values from 0 to 262143, as said below
- owner: int32 [128, 1024], P('lon', 'lat'), may hold values from 0 to 65535, as said below
- weight: int32 [128, 1024], P('lon', 'lat'), may hold values from 1 to 8
Outputs:
- spectra_out: float32 [1800, 128, 1024], P(None, 'lon', 'lat')
- wave_stress: float32 [2, 65536], P(None, ('lat', 'lon'))
- roughness: float32 [65536], P(('lat', 'lon'))
The draws below stay inside these ranges and needn't reach their ends.
Inputs may be any that keep to these rules, and one draw needn't show every extreme that they name: `spectra`: Positive. `wind_row`: A grid point in latitude band i (rows i * 128 to (i + 1) * 128 - 1) reads a row of band i: row // 32768 == i; any sector of the band. A grid point in latitude band i sends to a cell of band i: owner // 8192 == i; any sector of the band. Some cells receive no point.
All inputs are finite; a program needn't handle non-finite values. No bound on the sum of `sea_mask` on one device may be relied on, other than what follows from the above.
Results may differ from the reference program's by a relative error of at most 0.00024.
Values sent between devices are 32-bit elements; how exact they have to be, the bound alone decides.
No kernel may reach another device: no remote copies, remote signals or barrier semaphores. Data moves between devices by JAX's collectives and lax.ppermute only.
A program may use at most 256 MiB of HBM per device.

```python
import math
import jax
import jax.numpy as jnp
from jax import lax

NF = 50
ND = 36
PLON = 8
PLAT = 128
ATM_DEV = 2048
XC_DEV = 512
STEPS = 2
NLON = 128
NLAT = 1024
NB = 1800
ATM = 262144
XCELLS = 65536


def draw_spectra(key, part):
    key = jax.random.fold_in(key, 7)
    key_angle, key_peak, key_rough = jax.random.split(key, 3)
    index = jnp.arange(NB, dtype=jnp.int32)
    fpos = (index // ND).astype(jnp.float32)[:, None, None]
    dpos = (index % ND).astype(jnp.float32)[:, None, None]
    theta = 2.0 * math.pi * (dpos + 0.5) / ND
    center = jax.random.uniform(key_angle, (1, NLON, NLAT), jnp.float32, -math.pi, math.pi)
    peak = jax.random.uniform(key_peak, (1, NLON, NLAT), jnp.float32, 8.0, 16.0)
    rough = jnp.exp(jax.random.uniform(key_rough, (NB, NLON, NLAT), jnp.float32, math.log(0.5), math.log(2.0)))
    sharp = 4.0
    level = jnp.exp(-4.0 * math.log(1.07) * jnp.maximum(fpos - peak, 0.0))
    spread = 0.05 + jnp.exp(sharp * (jnp.cos(theta - center) - 1.0))
    return (level * spread * rough).astype(jnp.float32)


def draw_atm_wind(key, part):
    key = jax.random.fold_in(key, 5)
    key_speed, key_angle = jax.random.split(key)
    unit = jax.random.uniform(key_speed, (ATM,), jnp.float32, 0.0, 1.0)
    speed = 3.0 + 7.0 * unit
    angle = jax.random.uniform(key_angle, (ATM,), jnp.float32, -math.pi, math.pi)
    return jnp.stack([speed * jnp.cos(angle), speed * jnp.sin(angle)]).astype(jnp.float32)


def draw_wind_row(key, part):
    key = jax.random.fold_in(key, 11)
    sectors = NLON // PLON
    row = jnp.arange(NLAT, dtype=jnp.int32)[None, :]
    band = row // PLAT
    inside = jax.random.randint(key, (NLON, NLAT), 0, ATM_DEV * sectors, dtype=jnp.int32)
    return (band * sectors * ATM_DEV + inside).astype(jnp.int32)


def draw_owner(key, part):
    key = jax.random.fold_in(key, 23)
    sectors = NLON // PLON
    row = jnp.arange(NLAT, dtype=jnp.int32)[None, :]
    band = row // PLAT
    inside = jax.random.randint(key, (NLON, NLAT), 0, XC_DEV * sectors, dtype=jnp.int32)
    return (band * sectors * XC_DEV + inside).astype(jnp.int32)


def plant(array, rng, smallest, high):
    spot = [jax.random.randint(jax.random.fold_in(rng, axis), (), 0, length) for axis, length in enumerate(array.shape)]
    main_axis = array.shape.index(max(array.shape))
    next_to = spot[:main_axis] + [(spot[main_axis] + 1) % array.shape[main_axis]] + spot[main_axis + 1:]
    return array.at[tuple(spot)].set(smallest).at[tuple(next_to)].set(high)


def setup_inputs(seed: int = 0) -> dict:
    keys = jax.random.split(jax.random.key(seed), 7)
    spectra = draw_spectra(jax.random.fold_in(keys[6], 71), 0)
    sea_mask = plant((jax.random.randint(keys[1], (NLON, NLAT), 0, 4) < 3).astype(jnp.int32), jax.random.fold_in(keys[1], 1), 0, 1)
    atm_wind = draw_atm_wind(jax.random.fold_in(keys[6], 71), 0)
    wind_row = draw_wind_row(jax.random.fold_in(keys[6], 71), 0)
    owner = draw_owner(jax.random.fold_in(keys[6], 71), 0)
    weight = plant(jax.random.randint(keys[5], (NLON, NLAT), 1, 9), jax.random.fold_in(keys[5], 1), 1, 8).astype(jnp.int32)
    return dict(spectra=spectra, sea_mask=sea_mask, atm_wind=atm_wind, wind_row=wind_row, owner=owner, weight=weight)


def bin_tables(nfreq, ndir):
    index = jnp.arange(nfreq * ndir, dtype=jnp.int32)
    fpos = (index // ndir).astype(jnp.float32)
    dpos = (index % ndir).astype(jnp.float32)
    freq_b = 1.07 ** (fpos - (nfreq - 1))
    theta = 2.0 * math.pi * (dpos + 0.5) / ndir
    cos_b = jnp.cos(theta)
    sin_b = jnp.sin(theta)
    cour_b = 0.7 * (3.0 / 7.0) ** (fpos / (nfreq - 1))
    slope_b = 250.0 * freq_b ** 4 / ndir
    push_scale = 800.0 * freq_b ** 2 / ndir
    push_b = jnp.stack([push_scale * cos_b, push_scale * sin_b], axis=1)
    return (freq_b, cos_b, sin_b, cour_b, slope_b, push_b)

def wind_rate(wind_u, wind_v, freq_b, cos_b, sin_b):
    along = cos_b[:, None, None] * wind_u[None] + sin_b[:, None, None] * wind_v[None]
    return 0.2 * freq_b[:, None, None] * jnp.maximum(3.0 * freq_b[:, None, None] * along - 1.0, 0.0)

def force_terms(energy, rate_in, freq_b, msq):
    return energy * (1.0 + rate_in) / (1.0 + 4.0 * freq_b[:, None, None] * msq[None])

def advect(padded, cx_b, cy_b):
    center = padded[:, 1:-1, 1:-1]
    west = padded[:, :-2, 1:-1]
    east = padded[:, 2:, 1:-1]
    south = padded[:, 1:-1, :-2]
    north = padded[:, 1:-1, 2:]
    cxp = jnp.maximum(cx_b, 0.0)[:, None, None]
    cxm = jnp.minimum(cx_b, 0.0)[:, None, None]
    cyp = jnp.maximum(cy_b, 0.0)[:, None, None]
    cym = jnp.minimum(cy_b, 0.0)[:, None, None]
    return center - cxp * (center - west) - cxm * (east - center) - cyp * (center - south) - cym * (north - center)

def reference(spectra, sea_mask, atm_wind, wind_row, owner, weight):
    freq_b, cos_b, sin_b, cour_b, slope_b, push_b = bin_tables(NF, ND)
    maskf = sea_mask.astype(jnp.float32)
    wind_u = atm_wind[0][wind_row]
    wind_v = atm_wind[1][wind_row]
    xsize = spectra.shape[1]
    ysize = spectra.shape[2]
    energy = spectra * maskf[None]
    tables = (freq_b.reshape(NF, ND), cos_b.reshape(NF, ND), sin_b.reshape(NF, ND), cour_b.reshape(NF, ND))
    for step in range(STEPS):
        msq = jnp.einsum('bxy,b->xy', energy, slope_b, precision=lax.Precision.HIGHEST)

        def per_freq(args):
            block, fr, co, sn, cr = args
            rate = wind_rate(wind_u, wind_v, fr, co, sn)
            forced = force_terms(block, rate, fr, msq)
            padded = jnp.pad(forced, ((0, 0), (1, 1), (0, 0)), mode='wrap')
            padded = jnp.pad(padded, ((0, 0), (0, 0), (1, 1)))
            return advect(padded, cr * co, cr * sn) * maskf[None]
        energy = lax.map(per_freq, (energy.reshape(NF, ND, xsize, ysize),) + tables).reshape(NF * ND, xsize, ysize)

    def per_push(args):
        block, fr, co, sn, pb = args
        rate = wind_rate(wind_u, wind_v, fr, co, sn)
        return jnp.einsum('dxy,dk->kxy', rate * block, pb, precision=lax.Precision.HIGHEST)
    pushed = lax.map(per_push, (energy.reshape(NF, ND, xsize, ysize), tables[0], tables[1], tables[2], push_b.reshape(NF, ND, 2)))
    push = lax.optimization_barrier(jnp.sum(pushed, axis=0))
    share = weight.astype(jnp.float32) * maskf
    tau = 0.02 * (wind_u * wind_u + wind_v * wind_v) + 0.25
    terms = jnp.stack([share, share * tau, share * push[0], share * push[1]]).reshape(4, -1)
    sums = jnp.zeros((4, XCELLS), jnp.float32).at[:, owner.reshape(-1)].add(terms)
    total_w = jnp.maximum(sums[0], 1.0)
    wave_stress = sums[2:4] / total_w[None]
    ratio = (sums[2] * sums[2] + sums[3] * sums[3]) / jnp.maximum(sums[1], 1.0) ** 2
    roughness = jnp.sqrt(1.0 + ratio) * sums[1] / total_w
    return (energy, wave_stress, roughness)
```

```python
import functools
import math

import jax
import jax.numpy as jnp
import numpy as np
from jax import lax
from jax.experimental import pallas as pl
from jax.experimental.pallas import tpu as pltpu
from jax.sharding import PartitionSpec as P

NF = 50
ND = 36
HALF = 18
QUAD = 9
GROUPS = 10
FG = NF // GROUPS
GB = FG * ND
COL = 904
F32 = jnp.float32
BF16 = jnp.bfloat16

_f = np.arange(NF, dtype=np.float64)
_freq = 1.07 ** (_f - (NF - 1))
_theta = 2.0 * math.pi * (np.arange(ND) + 0.5) / ND
_cos = np.cos(_theta)
_sin = np.sin(_theta)
_gain = 0.6 * _freq**2
_base = 1.0 - 0.2 * _freq
_cour = 0.7 * (3.0 / 7.0) ** (_f / (NF - 1))
_slope = 250.0 * _freq**4 / ND
_four = 4.0 * _freq
_push = 800.0 * _freq**2 / ND
EASTWARD = list(range(0, 9)) + list(range(27, 36))
WESTWARD = list(range(9, 27))

SCAL = np.zeros((6, 64), np.float32)
for _i, _t in enumerate((_gain, _base, _cour, _slope, _four, _push)):
    SCAL[_i, :NF] = _t
SCAL = SCAL.reshape(-1)


def scal(sm, kind, f):
    return sm[kind * 64 + f]


def _lane_tables():
    tab = np.zeros((GROUPS, 8, 128), np.float32)
    tab[:, 1] = 1.0
    for g in range(GROUPS):
        for i in range(FG):
            f = g * FG + i
            for d in range(HALF):
                j = i * HALF + d
                tab[g, 0, j] = _gain[f]
                tab[g, 1, j] = _base[f]
                tab[g, 2, j] = _cos[d]
                tab[g, 3, j] = _sin[d]
                tab[g, 4, j] = _four[f]
    return tab


def _dir_tables():
    tab = np.zeros((4, HALF, 128), np.float32)
    for s, dirs in enumerate((EASTWARD, WESTWARD)):
        tab[2 * s] = _cos[dirs][:, None]
        tab[2 * s + 1] = _sin[dirs][:, None]
    return tab


LANE_TAB = _lane_tables()
DIR_TAB = _dir_tables()
FOUR_COL = np.broadcast_to(_four[:, None], (NF, 128)).astype(np.float32)


def quartets():
    for d in range(QUAD):
        yield (d, 17 - d, 18 + d, 35 - d)


def iota(shape, dim):
    return lax.broadcasted_iota(jnp.int32, shape, dim)


def pack_edges(ref, g, lane):
    edge_n = jnp.zeros((8, 128), F32)
    edge_s = jnp.zeros((8, 128), F32)
    for i in range(FG):
        for d in range(HALF):
            j = i * HALF + d
            e = ref[g * GB + i * ND + d]
            edge_n = jnp.where(lane == j, pltpu.roll(e, (j - 127) % 128, 1), edge_n)
            e = ref[g * GB + i * ND + HALF + d]
            edge_s = jnp.where(lane == j, pltpu.roll(e, j, 1) if j else e, edge_s)
    return edge_n, edge_s


def first_kernel(sm, spec_hbm, mask, wrow, spec, to_west, to_east, north, south, msq, sems):
    lane = iota((8, 128), 1)

    def copy(g):
        at = pl.ds(g * GB, GB)
        return pltpu.make_async_copy(spec_hbm.at[at], spec.at[at], sems.at[g])

    for g in range(GROUPS):
        copy(g).start()
    msq[...] = jnp.zeros_like(msq)

    @pl.loop(0, GROUPS)
    def _(g):
        copy(g).wait()
        total = jnp.zeros((8, 128), F32)
        for i in range(FG):
            acc = jnp.zeros((8, 128), F32)
            for d in range(ND):
                e = spec[g * GB + i * ND + d]
                acc = acc + e
                if d in WESTWARD:
                    k = i * HALF + WESTWARD.index(d)
                    for c in range(2):
                        to_west[pl.ds(c * COL + g * FG * HALF + k, 1), :] = e[c : c + 1]
                else:
                    k = i * HALF + EASTWARD.index(d)
                    for c in range(2):
                        to_east[pl.ds(c * COL + g * FG * HALF + k, 1), :] = e[6 + c : 7 + c]
            total = total + scal(sm, 3, g * FG + i) * acc
        msq[...] += total
        north[g], south[g] = pack_edges(spec, g, lane)

    maskf = mask[...].astype(F32)
    msq[...] = msq[...] * maskf
    rows = (msq[...], maskf, wrow[...].astype(F32))
    for c in range(2):
        for r, val in enumerate(rows):
            at = c * COL + 2 * GROUPS * FG * QUAD + r
            to_west[at : at + 1, :] = val[c : c + 1]
            to_east[at : at + 1, :] = val[6 + c : 7 + c]


SMEM = pl.BlockSpec(memory_space=pltpu.SMEM)
VMEM = pl.BlockSpec(memory_space=pltpu.VMEM)
ANY = pl.BlockSpec(memory_space=pl.ANY)
TILE = jax.ShapeDtypeStruct((8, 128), F32)
FIELD = jax.ShapeDtypeStruct((NF * ND, 8, 128), F32)
PARAMS = pltpu.CompilerParams(vmem_limit_bytes=56 * 2**20)


def first_call(spectra, mask, wrow):
    return pl.pallas_call(
        first_kernel,
        in_specs=[SMEM, ANY, VMEM, VMEM],
        out_specs=[VMEM] * 6,
        out_shape=[
            FIELD,
            jax.ShapeDtypeStruct((2 * COL, 128), F32),
            jax.ShapeDtypeStruct((2 * COL, 128), F32),
            jax.ShapeDtypeStruct((GROUPS, 8, 128), F32),
            jax.ShapeDtypeStruct((GROUPS, 8, 128), F32),
            TILE,
        ],
        scratch_shapes=[pltpu.SemaphoreType.DMA((GROUPS,))],
        compiler_params=PARAMS,
        name="first",
    )(jnp.asarray(SCAL), spectra, mask, wrow)


def split3(x):
    a = x.astype(BF16)
    r = x - a.astype(F32)
    b = r.astype(BF16)
    c = (r - b.astype(F32)).astype(BF16)
    return a, b, c


def wind_kernel(
    sm, table, wrow, msq, mask, west, east, north, south, lane_tab, dir_tab, four,
    u_ref, v_ref, side_ref, hx_w, hx_e, hp_w, hp_e, fn, fs,
):
    srcs, _, trows, _ = table.shape
    hi_count = srcs * trows
    rows = [wrow[x : x + 1, :] for x in range(8)]
    at = 2 * GROUPS * FG * QUAD
    for ref in (west, east):
        for c in range(2):
            rows.append(ref[c * COL + at + 2 : c * COL + at + 3, :].astype(jnp.int32))
    local = [r & (hi_count * 128 - 1) for r in rows]
    hi_iota = iota((hi_count, 128), 0)
    hot = jnp.concatenate(
        [jnp.where(hi_iota == (r // 128), 1.0, 0.0).astype(BF16) for r in local], axis=1
    )
    tab = jnp.concatenate(
        [table[:, c].reshape(hi_count, 128) for c in range(2)], axis=1
    )
    got = None
    for part in split3(tab):
        term = lax.dot_general(
            part, hot, (((0,), (0,)), ((), ())), preferred_element_type=F32
        )
        got = term if got is None else got + term
    lo_iota = iota((128, 128), 0)
    us, vs = [], []
    for n, r in enumerate(local):
        pick = lo_iota == (r & 127)
        us.append(jnp.sum(jnp.where(pick, got[0:128, n * 128 : n * 128 + 128], 0.0), axis=0, keepdims=True))
        vs.append(jnp.sum(jnp.where(pick, got[128:256, n * 128 : n * 128 + 128], 0.0), axis=0, keepdims=True))
    for x in range(8):
        u_ref[x : x + 1, :] = us[x]
        v_ref[x : x + 1, :] = vs[x]
    side_ref[0:1, :] = us[9]
    side_ref[1:2, :] = vs[9]
    side_ref[2:3, :] = west[COL + at + 1 : COL + at + 2, :]
    side_ref[3:4, :] = us[10]
    side_ref[4:5, :] = vs[10]
    side_ref[5:6, :] = east[at + 1 : at + 2, :]
    side_ref[6:8, :] = jnp.zeros((2, 128), F32)

    maskf = mask[...].astype(F32)
    for edge, out, lane, sign in ((north, fn, 127, 1.0), (south, fs, 0, -1.0)):
        pick = lambda a: jnp.broadcast_to(a[:, lane : lane + 1], (8, 128))
        ue, ve, me, qe = pick(u_ref[...]), pick(v_ref[...]), pick(maskf), pick(msq[...])
        for g in range(GROUPS):
            lt = lane_tab[g]
            along = sign * (lt[2:3] * ue + lt[3:4] * ve)
            t = jnp.maximum(lt[0:1] * along + lt[1:2], 1.0)
            out[g * 8 : g * 8 + 8, :] = edge[g] * t * (me / (1.0 + lt[4:5] * qe))

    row18 = iota((HALF, 128), 0)
    lane18 = iota((HALF, 128), 1)
    up = row18 < QUAD
    inner = lane18 != jnp.where(up, 0, 127)
    acc = {}
    for s, (ref, near, far, hx, hp) in enumerate(
        ((west, COL, 0, hx_w, hp_w), (east, 0, COL, hx_e, hp_e))
    ):
        cos = dir_tab[2 * s]
        sin = dir_tab[2 * s + 1]
        n_near, n_far = (9, 8) if s == 0 else (10, 11)
        al_near = cos * us[n_near] + sin * vs[n_near]
        al_far = cos * us[n_far] + sin * vs[n_far]
        fac = []
        for base in (near, far):
            q = ref[base + at : base + at + 1, :]
            m = ref[base + at + 1 : base + at + 2, :]
            fac.append(m / (1.0 + four[...] * q))
        acos = jnp.abs(cos)
        asin = jnp.abs(sin)
        for f in range(NF):
            a, b, cr = scal(sm, 0, f), scal(sm, 1, f), scal(sm, 2, f)
            g1 = ref[near + f * HALF : near + f * HALF + HALF, :]
            g2 = ref[far + f * HALF : far + f * HALF + HALF, :]
            g1 = g1 * jnp.maximum(a * al_near + b, 1.0) * fac[0][f : f + 1]
            g2 = g2 * jnp.maximum(a * al_far + b, 1.0) * fac[1][f : f + 1]
            hx[f] = g1
            kx = cr * acos
            ky = cr * asin
            rolled = jnp.where(up, pltpu.roll(g1, 1, 1), pltpu.roll(g1, 127, 1))
            hp[f] = (1.0 - kx - ky) * g1 + kx * g2 + jnp.where(inner, ky * rolled, 0.0)
            grp, i = f // FG, f % FG
            shift_n = i * HALF + (0 if s == 0 else QUAD)
            shift_s = i * HALF + (0 if s == 0 else -QUAD)
            cn = jnp.broadcast_to(g1[:, 127:128], (HALF, 128))
            cs = jnp.broadcast_to(g1[:, 0:1], (HALF, 128))
            cn = jnp.where(up & (lane18 == row18 + shift_n), cn, 0.0)
            cs = jnp.where(jnp.logical_not(up) & (lane18 == row18 + shift_s), cs, 0.0)
            for key, val in (("n", cn), ("s", cs)):
                have = acc.get((key, grp))
                acc[(key, grp)] = val if have is None else have + val
    for key, out in (("n", fn), ("s", fs)):
        for grp in range(GROUPS):
            out[80 + grp : 81 + grp, :] = jnp.sum(acc[(key, grp)], axis=0, keepdims=True)
        out[90:96, :] = jnp.zeros((6, 128), F32)


def wind_call(table, wrow, msq, mask, west, east, north, south):
    vmem = pl.BlockSpec(memory_space=pltpu.VMEM)
    halo = jax.ShapeDtypeStruct((NF, HALF, 128), F32)
    tile = jax.ShapeDtypeStruct((8, 128), F32)
    edge = jax.ShapeDtypeStruct((96, 128), F32)
    return pl.pallas_call(
        wind_kernel,
        in_specs=[pl.BlockSpec(memory_space=pltpu.SMEM)] + [vmem] * 11,
        out_specs=[vmem] * 9,
        out_shape=[tile, tile, tile, halo, halo, halo, halo, edge, edge],
        compiler_params=PARAMS,
        name="winds",
    )(
        jnp.asarray(SCAL), table, wrow, msq, mask, west, east, north, south,
        jnp.asarray(LANE_TAB), jnp.asarray(DIR_TAB), jnp.asarray(FOUR_COL),
    )


def along_table(along, u, v):
    for d in range(ND):
        along[d] = float(_cos[d]) * u + float(_sin[d]) * v


def shifted(gv, d, j, sub, lane, hx_w, hx_e, i, scale, halo_n, halo_s):
    if d in WESTWARD:
        k = WESTWARD.index(d)
        row = hx_e[i, k : k + 1, :]
        row = jnp.broadcast_to(row if scale is None else row * scale[1], (8, 128))
        xs = jnp.where(sub == 7, row, pltpu.roll(gv, 7, 0))
    else:
        k = EASTWARD.index(d)
        row = hx_w[i, k : k + 1, :]
        row = jnp.broadcast_to(row if scale is None else row * scale[0], (8, 128))
        xs = jnp.where(sub == 0, row, pltpu.roll(gv, 1, 0))
    if d < HALF:
        halo = pltpu.roll(halo_n, (-j) % 128, 1) if j else halo_n
        ys = jnp.where(lane == 0, halo, pltpu.roll(gv, 1, 1))
    else:
        halo = pltpu.roll(halo_s, 127 - j, 1)
        ys = jnp.where(lane == 127, halo, pltpu.roll(gv, 127, 1))
    return xs, ys


def step_one_kernel(
    sm, spec, u, v, msq, mask, hx_w, hx_e, rn, rs, lane_tab,
    out, msq2, fn2, fs2, along, edges_n, edges_s,
):
    lane = iota((8, 128), 1)
    sub = iota((8, 128), 0)
    maskf = mask[...].astype(F32)
    along_table(along, u[...], v[...])
    msq2[...] = jnp.zeros_like(msq2)

    @pl.loop(0, GROUPS)
    def _(g):
        total = jnp.zeros((8, 128), F32)
        at = pl.ds(pl.multiple_of(g * 8, 8), 8)
        halo_n = rn[at, :]
        halo_s = rs[at, :]
        for i in range(FG):
            f = g * FG + i
            a, b, cr = scal(sm, 0, f), scal(sm, 1, f), scal(sm, 2, f)
            fac = maskf / (1.0 + scal(sm, 4, f) * msq[...])
            acc = jnp.zeros((8, 128), F32)
            for quartet in quartets():
                d0 = quartet[0]
                kx = cr * float(abs(_cos[d0]))
                ky = cr * float(abs(_sin[d0]))
                k0 = 1.0 - kx - ky
                for d in quartet:
                    j = i * HALF + d % HALF
                    gv = spec[f * ND + d] * jnp.maximum(a * along[d] + b, 1.0) * fac
                    xs, ys = shifted(gv, d, j, sub, lane, hx_w, hx_e, f, None, halo_n, halo_s)
                    e = k0 * gv + kx * xs + ky * ys
                    out[f * ND + d] = e
                    acc = acc + e
            total = total + scal(sm, 3, f) * acc
        msq2[...] += total

    @pl.loop(0, GROUPS)
    def _(g):
        edges_n[g], edges_s[g] = pack_edges(out, g, lane)

    msq2[...] = msq2[...] * maskf
    for edge, dst, at, sign in ((edges_n, fn2, 127, 1.0), (edges_s, fs2, 0, -1.0)):
        pick = lambda z: jnp.broadcast_to(z[:, at : at + 1], (8, 128))
        ue, ve, me, qe = pick(u[...]), pick(v[...]), pick(maskf), pick(msq2[...])
        for q in range(GROUPS):
            lt = lane_tab[q]
            al = sign * (lt[2:3] * ue + lt[3:4] * ve)
            t = jnp.maximum(lt[0:1] * al + lt[1:2], 1.0)
            dst[q * 8 : q * 8 + 8, :] = edge[q] * t * (me / (1.0 + lt[4:5] * qe))


def step_one_call(spectra, u, v, msq, mask, hx_w, hx_e, rn, rs):
    return pl.pallas_call(
        step_one_kernel,
        in_specs=[SMEM] + [VMEM] * 10,
        out_specs=[VMEM] * 4,
        out_shape=[
            FIELD,
            TILE,
            jax.ShapeDtypeStruct((80, 128), F32),
            jax.ShapeDtypeStruct((80, 128), F32),
        ],
        scratch_shapes=[
            pltpu.VMEM((ND, 8, 128), F32),
            pltpu.VMEM((GROUPS, 8, 128), F32),
            pltpu.VMEM((GROUPS, 8, 128), F32),
        ],
        compiler_params=PARAMS,
        name="step_one",
    )(jnp.asarray(SCAL), spectra, u, v, msq, mask, hx_w, hx_e, rn, rs, jnp.asarray(LANE_TAB))


def halo_kernel(sm, hp_w, hp_e, rn, rs, side, dir_tab, hq_w, hq_e):
    row18 = iota((HALF, 128), 0)
    lane18 = iota((HALF, 128), 1)
    up = row18 < QUAD
    place = lane18 == jnp.where(up, 0, 127)
    for s, (hp, hq) in enumerate(((hp_w, hq_w), (hp_e, hq_e))):
        cos = dir_tab[2 * s]
        sin = dir_tab[2 * s + 1]
        asin = jnp.abs(sin)
        along = cos * side[3 * s : 3 * s + 1, :] + sin * side[3 * s + 1 : 3 * s + 2, :]
        for f in range(NF):
            a, b, cr = scal(sm, 0, f), scal(sm, 1, f), scal(sm, 2, f)
            grp, i = f // FG, f % FG
            shift = jnp.where(up, i * HALF + (0 if s == 0 else QUAD), i * HALF + (0 if s == 0 else -QUAD))
            src = jnp.where(up, rn[80 + grp : 81 + grp, :], rs[80 + grp : 81 + grp, :])
            col = jnp.sum(jnp.where(lane18 == row18 + shift, src, 0.0), axis=1, keepdims=True)
            e = hp[f] + jnp.where(place, (cr * asin) * col, 0.0)
            hq[f] = e * jnp.maximum(a * along + b, 1.0)


def halo_call(hp_w, hp_e, rn, rs, side):
    vmem = pl.BlockSpec(memory_space=pltpu.VMEM)
    halo = jax.ShapeDtypeStruct((NF, HALF, 128), F32)
    return pl.pallas_call(
        halo_kernel,
        in_specs=[pl.BlockSpec(memory_space=pltpu.SMEM)] + [vmem] * 6,
        out_specs=[vmem] * 2,
        out_shape=[halo, halo],
        compiler_params=PARAMS,
        name="halo_columns",
    )(jnp.asarray(SCAL), hp_w, hp_e, rn, rs, side, jnp.asarray(DIR_TAB))


def step_two_kernel(
    sm, spec, u, v, msq, mask, msq_w, msq_e, side, hq_w, hq_e, rn, rs, owner, weight,
    out, cells, along, push, field, sems,
):
    lane = iota((8, 128), 1)
    sub = iota((8, 128), 0)
    maskf = mask[...].astype(F32)
    along_table(along, u[...], v[...])
    push[...] = jnp.zeros_like(push)

    def copy(g):
        at = pl.ds(g * GB, GB)
        return pltpu.make_async_copy(field.at[at], out.at[at], sems.at[g])

    @pl.loop(0, GROUPS)
    def _(g):
        pu = jnp.zeros((8, 128), F32)
        pv = jnp.zeros((8, 128), F32)
        at = pl.ds(pl.multiple_of(g * 8, 8), 8)
        halo_n = rn[at, :]
        halo_s = rs[at, :]
        for i in range(FG):
            f = g * FG + i
            a, b, cr, four = scal(sm, 0, f), scal(sm, 1, f), scal(sm, 2, f), scal(sm, 4, f)
            fac = maskf / (1.0 + four * msq[...])
            scale = (
                side[2:3, :] / (1.0 + four * msq_w[7:8, :]),
                side[5:6, :] / (1.0 + four * msq_e[0:1, :]),
            )
            fu = jnp.zeros((8, 128), F32)
            fv = jnp.zeros((8, 128), F32)
            for quartet in quartets():
                d0 = quartet[0]
                kx = cr * float(abs(_cos[d0]))
                ky = cr * float(abs(_sin[d0]))
                k0 = 1.0 - kx - ky
                q = []
                for d in quartet:
                    j = i * HALF + d % HALF
                    t = jnp.maximum(a * along[d] + b, 1.0)
                    gv = spec[f * ND + d] * t * fac
                    xs, ys = shifted(gv, d, j, sub, lane, hq_w, hq_e, f, scale, halo_n, halo_s)
                    e = (k0 * gv + kx * xs + ky * ys) * maskf
                    field[f * ND + d] = e
                    q.append((t - 1.0) * e)
                lo = q[0] - q[2]
                hi = q[1] - q[3]
                fu = fu + float(_cos[d0]) * (lo - hi)
                fv = fv + float(_sin[d0]) * (lo + hi)
            pu = pu + scal(sm, 5, f) * fu
            pv = pv + scal(sm, 5, f) * fv
        push[0] += pu
        push[1] += pv
        copy(g).start()

    def finish():
        uu, vv = u[...], v[...]
        share = weight[...].astype(F32) * maskf
        tau = 0.02 * (uu * uu + vv * vv) + 0.25
        terms = (share, share * tau, share * push[0], share * push[1])
        parts = [split3(t) for t in terms]
        dests = cells.shape[0]
        own = owner[...] & (dests * 512 - 1)
        hi_own = own // 128
        lo_own = own & 127
        row = iota((dests * 16, 128), 0)
        want = (row // 16) * 4 + row % 4
        lo_iota = iota((128, 128), 0)
        kind = iota((16, 128), 0) // 4
        total = jnp.zeros((dests * 16, 128), F32)
        for x in range(8):
            hot = jnp.where(lo_iota == lo_own[x : x + 1], 1.0, 0.0).astype(BF16)
            match = want == hi_own[x : x + 1]
            for p in range(3):
                rows = [parts[k][p][x : x + 1].astype(F32) for k in range(4)]
                tile = jnp.where(
                    kind == 0, rows[0],
                    jnp.where(kind == 1, rows[1], jnp.where(kind == 2, rows[2], rows[3])),
                )
                lhs = jnp.where(match, jnp.concatenate([tile] * dests, axis=0), 0.0).astype(BF16)
                total = total + lax.dot_general(
                    lhs, hot, (((1,), (1,)), ((), ())), preferred_element_type=F32
                )
        cells[...] = total.reshape(dests, 16, 128)

    finish()
    for g in range(GROUPS):
        copy(g).wait()


def step_two_call(spec, u, v, msq, mask, msq_w, msq_e, side, hq_w, hq_e, rn, rs, owner, weight, dests):
    return pl.pallas_call(
        step_two_kernel,
        in_specs=[SMEM] + [VMEM] * 14,
        out_specs=[ANY, VMEM],
        out_shape=[FIELD, jax.ShapeDtypeStruct((dests, 16, 128), F32)],
        scratch_shapes=[
            pltpu.VMEM((ND, 8, 128), F32),
            pltpu.VMEM((2, 8, 128), F32),
            pltpu.VMEM((NF * ND, 8, 128), F32),
            pltpu.SemaphoreType.DMA((GROUPS,)),
        ],
        compiler_params=PARAMS,
        name="step_two",
    )(
        jnp.asarray(SCAL), spec, u, v, msq, mask, msq_w, msq_e, side, hq_w, hq_e, rn, rs,
        owner, weight,
    )


def cell_kernel(parts, stress, rough):
    sums = jnp.sum(parts[...], axis=0)
    w, a, bx, by = (sums[4 * k : 4 * k + 4] for k in range(4))
    total_w = jnp.maximum(w, 1.0)
    sx = bx / total_w
    sy = by / total_w
    low = jnp.maximum(a, 1.0)
    r = jnp.sqrt(1.0 + (bx * bx + by * by) / (low * low)) * a / total_w
    for n in range(4):
        at = slice(n * 128, n * 128 + 128)
        stress[0:1, at] = sx[n : n + 1]
        stress[1:2, at] = sy[n : n + 1]
        rough[0:1, at] = r[n : n + 1]


def cell_call(parts):
    return pl.pallas_call(
        cell_kernel,
        out_shape=[jax.ShapeDtypeStruct((2, 512), F32), jax.ShapeDtypeStruct((1, 512), F32)],
        name="cells",
    )(parts)


def body(spectra, sea_mask, atm_wind, wind_row, owner, weight):
    lons = lax.axis_size("lon")
    lats = lax.axis_size("lat")
    eastward = [(i, (i + 1) % lons) for i in range(lons)]
    westward = [(i, (i - 1) % lons) for i in range(lons)]
    northward = [(i, i + 1) for i in range(lats - 1)]
    southward = [(i + 1, i) for i in range(lats - 1)]

    spectra, to_west, to_east, north, south, msq1 = first_call(spectra, sea_mask, wind_row)
    from_west = lax.ppermute(to_east, "lon", eastward)
    from_east = lax.ppermute(to_west, "lon", westward)
    rows = atm_wind.reshape(1, 2, 16, 128)
    table = lax.all_to_all(jnp.broadcast_to(rows, (lons, 2, 16, 128)), "lon", 0, 0)
    u, v, side, hx_w, hx_e, hp_w, hp_e, fn, fs = wind_call(
        table, wind_row, msq1, sea_mask, from_west, from_east, north, south
    )
    rn = lax.ppermute(fn, "lat", northward)
    rs = lax.ppermute(fs, "lat", southward)
    energy, msq2, fn2, fs2 = step_one_call(
        spectra, u, v, msq1, sea_mask, hx_w, hx_e, rn, rs
    )
    rn2 = lax.ppermute(fn2, "lat", northward)
    rs2 = lax.ppermute(fs2, "lat", southward)
    msq_w = lax.ppermute(msq2, "lon", eastward)
    msq_e = lax.ppermute(msq2, "lon", westward)
    hq_w, hq_e = halo_call(hp_w, hp_e, rn, rs, side)
    energy, cells = step_two_call(
        energy, u, v, msq2, sea_mask, msq_w, msq_e, side, hq_w, hq_e, rn2, rs2,
        owner, weight, lons,
    )
    parts = lax.all_to_all(cells, "lon", 0, 0)
    stress, rough = cell_call(parts)
    return energy, stress, rough.reshape(512)


def solution(mesh):
    in_specs = (
        P(None, "lon", "lat"),
        P("lon", "lat"),
        P(None, ("lat", "lon")),
        P("lon", "lat"),
        P("lon", "lat"),
        P("lon", "lat"),
    )
    out_specs = (P(None, "lon", "lat"), P(None, ("lat", "lon")), P(("lat", "lon")))
    return jax.shard_map(body, mesh=mesh, in_specs=in_specs, out_specs=out_specs, check_vma=False)
```

```python
import functools
import math

import jax
import jax.numpy as jnp
import numpy as np
from jax import lax
from jax.experimental import pallas as pl
from jax.experimental.pallas import tpu as pltpu
from jax.sharding import PartitionSpec as P

NF = 50
ND = 36
HALF = 18
QUAD = 9
GROUPS = 10
FG = NF // GROUPS
GB = FG * ND
ROWS = NF * HALF
COL = ROWS + 4
F32 = jnp.float32
BF16 = jnp.bfloat16

_f = np.arange(NF, dtype=np.float64)
_freq = 1.07 ** (_f - (NF - 1))
_theta = 2.0 * math.pi * (np.arange(ND) + 0.5) / ND
_cos = np.cos(_theta)
_sin = np.sin(_theta)
_gain = 0.6 * _freq**2
_base = 1.0 - 0.2 * _freq
_cour = 0.7 * (3.0 / 7.0) ** (_f / (NF - 1))
_slope = 250.0 * _freq**4 / ND
_four = 4.0 * _freq
_push = 800.0 * _freq**2 / ND
EASTWARD = list(range(0, 9)) + list(range(27, 36))
WESTWARD = list(range(9, 27))

SCAL = np.zeros((6, 64), np.float32)
for _i, _t in enumerate((_gain, _base, _cour, _slope, _four, _push)):
    SCAL[_i, :NF] = _t
SCAL = SCAL.reshape(-1)


def scal(sm, kind, f):
    return sm[kind * 64 + f]


def _lane_tables():
    tab = np.zeros((GROUPS, 8, 128), np.float32)
    tab[:, 1] = 1.0
    for g in range(GROUPS):
        for i in range(FG):
            f = g * FG + i
            for d in range(HALF):
                j = i * HALF + d
                tab[g, 0, j] = _gain[f]
                tab[g, 1, j] = _base[f]
                tab[g, 2, j] = _cos[d]
                tab[g, 3, j] = _sin[d]
                tab[g, 4, j] = _four[f]
    return tab


def _dir_tables():
    tab = np.zeros((4, HALF, 128), np.float32)
    for s, dirs in enumerate((EASTWARD, WESTWARD)):
        tab[2 * s] = _cos[dirs][:, None]
        tab[2 * s + 1] = _sin[dirs][:, None]
    return tab


LANE_TAB = _lane_tables()
DIR_TAB = _dir_tables()
FOUR_COL = np.broadcast_to(_four[:, None], (NF, 128)).astype(np.float32)


def quartets():
    for d in range(QUAD):
        yield (d, 17 - d, 18 + d, 35 - d)


def iota(shape, dim):
    return lax.broadcasted_iota(jnp.int32, shape, dim)


def pack_edges(ref, g, lane):
    edge_n = jnp.zeros((8, 128), F32)
    edge_s = jnp.zeros((8, 128), F32)
    for i in range(FG):
        for d in range(HALF):
            j = i * HALF + d
            e = ref[g * GB + i * ND + d]
            edge_n = jnp.where(lane == j, pltpu.roll(e, (j - 127) % 128, 1), edge_n)
            e = ref[g * GB + i * ND + HALF + d]
            edge_s = jnp.where(lane == j, pltpu.roll(e, j, 1) if j else e, edge_s)
    return edge_n, edge_s


def first_kernel(spec_hbm, near_w, near_e, north, south, msq, spec, sems):
    lane = iota((8, 128), 1)

    def copy(g):
        at = pl.ds(g * GB, GB)
        return pltpu.make_async_copy(spec_hbm.at[at], spec.at[at], sems.at[g])

    for g in range(GROUPS):
        copy(g).start()
    msq[...] = jnp.zeros_like(msq)

    def group(g, growth):
        copy(g).wait()
        total = jnp.zeros((8, 128), F32)
        for i in range(FG):
            acc = jnp.zeros((8, 128), F32)
            for d in range(ND):
                e = spec[g * GB + i * ND + d]
                acc = acc + e
                if d in WESTWARD:
                    k = pl.ds(g * FG * HALF + i * HALF + WESTWARD.index(d), 1)
                    near_w[k, :] = e[0:1]
                else:
                    k = pl.ds(g * FG * HALF + i * HALF + EASTWARD.index(d), 1)
                    near_e[k, :] = e[7:8]
            total = total + float(_slope[i]) * acc
        msq[...] += growth * total
        north[g], south[g] = pack_edges(spec, g, lane)
        return growth * float(_slope[FG] / _slope[0])

    lax.fori_loop(0, GROUPS, group, jnp.float32(1.0))
    q = msq[...]
    for near, x in ((near_w, 0), (near_e, 7)):
        near[ROWS : ROWS + 1, :] = q[x : x + 1]
        near[ROWS + 1 : COL, :] = jnp.zeros((COL - ROWS - 1, 128), F32)


def sector_kernel(mask, winds, wrow, mine):
    for c in range(2):
        for r in range(16):
            mine[0, 16 * c + r : 16 * c + r + 1, :] = winds[c : c + 1, 128 * r : 128 * r + 128]
    mine[0, 32:40, :] = wrow[...].astype(F32)
    mine[0, 40:48, :] = mask[...].astype(F32)
    rows = mine[0]
    for n in range(1, mine.shape[0]):
        mine[n] = rows


SMEM = pl.BlockSpec(memory_space=pltpu.SMEM)
VMEM = pl.BlockSpec(memory_space=pltpu.VMEM)
HBM = pl.BlockSpec(memory_space=pltpu.HBM)
TILE = jax.ShapeDtypeStruct((8, 128), F32)
FIELD = jax.ShapeDtypeStruct((NF * ND, 8, 128), F32)
BUFFER = pltpu.VMEM((NF * ND, 8, 128), F32)
PARAMS = pltpu.CompilerParams(vmem_limit_bytes=30 * 2**20)
MIDDLE = pltpu.CompilerParams(vmem_limit_bytes=43 * 2**20)
WIDE = pltpu.CompilerParams(vmem_limit_bytes=48 * 2**20)
ALONE = pltpu.CompilerParams(vmem_limit_bytes=54 * 2**20)


def first_call(spectra):
    edge = jax.ShapeDtypeStruct((COL, 128), F32)
    pack = jax.ShapeDtypeStruct((GROUPS, 8, 128), F32)
    return pl.pallas_call(
        first_kernel,
        in_specs=[HBM],
        out_specs=[VMEM] * 5,
        out_shape=[edge, edge, pack, pack, TILE],
        scratch_shapes=[BUFFER, pltpu.SemaphoreType.DMA((GROUPS,))],
        compiler_params=WIDE,
        name="first",
    )(spectra)


def sector_call(mask, winds, wrow, lons):
    return pl.pallas_call(
        sector_kernel,
        in_specs=[VMEM] * 3,
        out_specs=VMEM,
        out_shape=jax.ShapeDtypeStruct((lons, 48, 128), F32),
        compiler_params=ALONE,
        name="sector",
    )(mask, winds, wrow)


def split3(x):
    a = x.astype(BF16)
    r = x - a.astype(F32)
    b = r.astype(BF16)
    c = (r - b.astype(F32)).astype(BF16)
    return a, b, c


def wind_kernel(
    me_ref, table, wrow, msq, mask, north, south, lane_tab,
    u_ref, v_ref, side_ref, fn, fs,
):
    srcs = table.shape[0]
    me = me_ref[0]
    hi_count = srcs * 16
    west = table.at[(me + srcs - 1) & (srcs - 1)]
    east = table.at[(me + 1) & (srcs - 1)]
    rows = [wrow[x : x + 1, :] for x in range(8)]
    for ref, x in ((west, 7), (east, 0)):
        rows.append(ref[32 + x : 33 + x, :].astype(jnp.int32))
    local = [r & (hi_count * 128 - 1) for r in rows]
    hi_iota = iota((hi_count, 128), 0)
    hots = []
    for r in local:
        hots.append(jnp.where(hi_iota == r // 128, 1.0, 0.0).astype(BF16))
    hot = jnp.concatenate(hots, axis=1)
    tab = jnp.concatenate(
        [table[:, 16 * c : 16 * c + 16].reshape(hi_count, 128) for c in range(2)], axis=1
    )
    got = None
    for part in split3(tab):
        term = lax.dot_general(
            part, hot, (((0,), (0,)), ((), ())), preferred_element_type=F32
        )
        got = term if got is None else got + term
    lo_iota = iota((128, 128), 0)
    us, vs = [], []
    for n, r in enumerate(local):
        pick = lo_iota == (r & 127)
        at = slice(n * 128, n * 128 + 128)
        us.append(jnp.sum(jnp.where(pick, got[0:128, at], 0.0), axis=0, keepdims=True))
        vs.append(jnp.sum(jnp.where(pick, got[128:256, at], 0.0), axis=0, keepdims=True))
    for x in range(8):
        u_ref[x : x + 1, :] = us[x]
        v_ref[x : x + 1, :] = vs[x]
    for n, (ref, x) in enumerate(((west, 7), (east, 0))):
        side_ref[3 * n : 3 * n + 1, :] = us[8 + n]
        side_ref[3 * n + 1 : 3 * n + 2, :] = vs[8 + n]
        side_ref[3 * n + 2 : 3 * n + 3, :] = ref[40 + x : 41 + x, :]
    side_ref[6:8, :] = jnp.zeros((2, 128), F32)

    maskf = mask[...].astype(F32)
    for edge, out, lane, sign in ((north, fn, 127, 1.0), (south, fs, 0, -1.0)):
        pick = lambda a: jnp.broadcast_to(a[:, lane : lane + 1], (8, 128))
        ue, ve, me_, qe = pick(u_ref[...]), pick(v_ref[...]), pick(maskf), pick(msq[...])
        for g in range(GROUPS):
            lt = lane_tab[g]
            along = sign * (lt[2:3] * ue + lt[3:4] * ve)
            t = jnp.maximum(lt[0:1] * along + lt[1:2], 1.0)
            out[g * 8 : g * 8 + 8, :] = edge[g] * t * (me_ / (1.0 + lt[4:5] * qe))


def wind_call(me, table, wrow, msq, mask, north, south):
    edge = jax.ShapeDtypeStruct((80, 128), F32)
    return pl.pallas_call(
        wind_kernel,
        in_specs=[SMEM] + [VMEM] * 7,
        out_specs=[VMEM] * 5,
        out_shape=[TILE, TILE, TILE, edge, edge],
        compiler_params=PARAMS,
        name="winds",
    )(me, table, wrow, msq, mask, north, south, jnp.asarray(LANE_TAB))


def forced_column(sm, src, dst, s, u_row, v_row, mask_row, msq_row, dir_tab, four):
    along = dir_tab[2 * s] * u_row + dir_tab[2 * s + 1] * v_row
    fac = mask_row / (1.0 + four[...] * msq_row)
    for f in range(NF):
        at = slice(f * HALF, f * HALF + HALF)
        t = jnp.maximum(scal(sm, 0, f) * along + scal(sm, 1, f), 1.0)
        dst[at, :] = src[at, :] * t * fac[f : f + 1]


def along_table(along, u, v):
    for d in range(ND):
        along[d] = float(_cos[d]) * u + float(_sin[d]) * v


def shifted(gv, d, j, sub, lane, hx_w, hx_e, row0, halo_n, halo_s):
    if d in WESTWARD:
        k = WESTWARD.index(d)
        row = hx_e[pl.ds(row0 + k, 1), :]
        row = jnp.broadcast_to(row, (8, 128))
        xs = jnp.where(sub == 7, row, pltpu.roll(gv, 7, 0))
    else:
        k = EASTWARD.index(d)
        row = hx_w[pl.ds(row0 + k, 1), :]
        row = jnp.broadcast_to(row, (8, 128))
        xs = jnp.where(sub == 0, row, pltpu.roll(gv, 1, 0))
    if d < HALF:
        halo = pltpu.roll(halo_n, (-j) % 128, 1) if j else halo_n
        ys = jnp.where(lane == 0, halo, pltpu.roll(gv, 1, 1))
    else:
        halo = pltpu.roll(halo_s, 127 - j, 1)
        ys = jnp.where(lane == 127, halo, pltpu.roll(gv, 127, 1))
    return xs, ys


def step_one_kernel(
    sm, spec_hbm, u, v, msq, mask, near_w, near_e, side, rn, rs, lane_tab, dir_tab, four_tab,
    out, msq2, fn2, fs2, to_w, to_e, spec, along, edges_n, edges_s, hx_w, hx_e, sems,
):
    def copy(g):
        at = pl.ds(g * GB, GB)
        return pltpu.make_async_copy(spec_hbm.at[at], spec.at[at], sems.at[g])

    for g in range(GROUPS):
        copy(g).start()
    for s, near, hx in ((0, near_w, hx_w), (1, near_e, hx_e)):
        rows = (side[3 * s + r : 3 * s + r + 1, :] for r in range(3))
        forced_column(sm, near, hx, s, *rows, near[ROWS : ROWS + 1, :], dir_tab, four_tab)
    lane = iota((8, 128), 1)
    sub = iota((8, 128), 0)
    maskf = mask[...].astype(F32)
    along_table(along, u[...], v[...])
    msq2[...] = jnp.zeros_like(msq2)

    @pl.loop(0, GROUPS)
    def _(g):
        copy(g).wait()
        last = jnp.maximum(g - 1, 0)
        edges_n[last], edges_s[last] = pack_edges(out, last, lane)
        total = jnp.zeros((8, 128), F32)
        at = pl.ds(pl.multiple_of(g * 8, 8), 8)
        halo_n = rn[at, :]
        halo_s = rs[at, :]
        for i in range(FG):
            f = g * FG + i
            a, b, cr = scal(sm, 0, f), scal(sm, 1, f), scal(sm, 2, f)
            fac = maskf / (1.0 + scal(sm, 4, f) * msq[...])
            acc = jnp.zeros((8, 128), F32)
            for quartet in quartets():
                d0 = quartet[0]
                kx = cr * float(abs(_cos[d0]))
                ky = cr * float(abs(_sin[d0]))
                k0 = 1.0 - kx - ky
                for d in quartet:
                    j = i * HALF + d % HALF
                    gv = spec[f * ND + d] * jnp.maximum(a * along[d] + b, 1.0) * fac
                    xs, ys = shifted(gv, d, j, sub, lane, hx_w, hx_e, f * HALF, halo_n, halo_s)
                    e = k0 * gv + kx * xs + ky * ys
                    out[f * ND + d] = e
                    acc = acc + e
                    if d in WESTWARD:
                        to_w[pl.ds(f * HALF + WESTWARD.index(d), 1), :] = e[0:1]
                    else:
                        to_e[pl.ds(f * HALF + EASTWARD.index(d), 1), :] = e[7:8]
            total = total + scal(sm, 3, f) * acc
        msq2[...] += total

    edges_n[GROUPS - 1], edges_s[GROUPS - 1] = pack_edges(out, GROUPS - 1, lane)

    msq2[...] = msq2[...] * maskf
    for edge, dst, at, sign in ((edges_n, fn2, 127, 1.0), (edges_s, fs2, 0, -1.0)):
        pick = lambda z: jnp.broadcast_to(z[:, at : at + 1], (8, 128))
        ue, ve, me, qe = pick(u[...]), pick(v[...]), pick(maskf), pick(msq2[...])
        for q in range(GROUPS):
            lt = lane_tab[q]
            al = sign * (lt[2:3] * ue + lt[3:4] * ve)
            t = jnp.maximum(lt[0:1] * al + lt[1:2], 1.0)
            dst[q * 8 : q * 8 + 8, :] = edge[q] * t * (me / (1.0 + lt[4:5] * qe))
    for s, col, x in ((0, to_e, 7), (1, to_w, 0)):
        rows = (z[x : x + 1] for z in (u[...], v[...], maskf, msq2[...]))
        forced_column(sm, col, col, s, *rows, dir_tab, four_tab)
        col[ROWS:COL, :] = jnp.zeros((COL - ROWS, 128), F32)


def step_one_call(spectra, u, v, msq, mask, near_w, near_e, side, rn, rs):
    edge = jax.ShapeDtypeStruct((80, 128), F32)
    column = jax.ShapeDtypeStruct((COL, 128), F32)
    return pl.pallas_call(
        step_one_kernel,
        in_specs=[SMEM, HBM] + [VMEM] * 12,
        out_specs=[VMEM] * 6,
        out_shape=[FIELD, TILE, edge, edge, column, column],
        scratch_shapes=[
            BUFFER,
            pltpu.VMEM((ND, 8, 128), F32),
            pltpu.VMEM((GROUPS, 8, 128), F32),
            pltpu.VMEM((GROUPS, 8, 128), F32),
            pltpu.VMEM((COL, 128), F32),
            pltpu.VMEM((COL, 128), F32),
            pltpu.SemaphoreType.DMA((GROUPS,)),
        ],
        compiler_params=MIDDLE,
        name="step_one",
    )(
        jnp.asarray(SCAL), spectra, u, v, msq, mask, near_w, near_e, side, rn, rs,
        jnp.asarray(LANE_TAB), jnp.asarray(DIR_TAB), jnp.asarray(FOUR_COL),
    )


def step_two_kernel(
    sm, spec, u, v, msq, mask, hq_w, hq_e, rn, rs, owner, weight,
    out, cells, along, push, field, sems,
):
    lane = iota((8, 128), 1)
    sub = iota((8, 128), 0)
    maskf = mask[...].astype(F32)
    along_table(along, u[...], v[...])
    push[...] = jnp.zeros_like(push)

    def copy(g):
        at = pl.ds(g * GB, GB)
        return pltpu.make_async_copy(field.at[at], out.at[at], sems.at[g])

    @pl.loop(0, GROUPS)
    def _(g):
        pu = jnp.zeros((8, 128), F32)
        pv = jnp.zeros((8, 128), F32)
        at = pl.ds(pl.multiple_of(g * 8, 8), 8)
        halo_n = rn[at, :]
        halo_s = rs[at, :]
        for i in range(FG):
            f = g * FG + i
            a, b, cr, four = scal(sm, 0, f), scal(sm, 1, f), scal(sm, 2, f), scal(sm, 4, f)
            fac = maskf / (1.0 + four * msq[...])
            fu = jnp.zeros((8, 128), F32)
            fv = jnp.zeros((8, 128), F32)
            for quartet in quartets():
                d0 = quartet[0]
                kx = cr * float(abs(_cos[d0]))
                ky = cr * float(abs(_sin[d0]))
                k0 = 1.0 - kx - ky
                q = []
                for d in quartet:
                    j = i * HALF + d % HALF
                    t = jnp.maximum(a * along[d] + b, 1.0)
                    gv = spec[f * ND + d] * t * fac
                    xs, ys = shifted(gv, d, j, sub, lane, hq_w, hq_e, f * HALF, halo_n, halo_s)
                    e = (k0 * gv + kx * xs + ky * ys) * maskf
                    field[f * ND + d] = e
                    q.append((t - 1.0) * e)
                lo = q[0] - q[2]
                hi = q[1] - q[3]
                fu = fu + float(_cos[d0]) * (lo - hi)
                fv = fv + float(_sin[d0]) * (lo + hi)
            pu = pu + scal(sm, 5, f) * fu
            pv = pv + scal(sm, 5, f) * fv
        push[0] += pu
        push[1] += pv
        copy(g).start()

    def finish():
        uu, vv = u[...], v[...]
        share = weight[...].astype(F32) * maskf
        tau = 0.02 * (uu * uu + vv * vv) + 0.25
        terms = (share, share * tau, share * push[0], share * push[1])
        parts = [split3(t) for t in terms]
        dests = cells.shape[0]
        own = owner[...] & (dests * 512 - 1)
        hi_own = own // 128
        lo_own = own & 127
        row = iota((dests * 16, 128), 0)
        want = (row // 16) * 4 + row % 4
        lo_iota = iota((128, 128), 0)
        kind = iota((16, 128), 0) // 4
        total = jnp.zeros((dests * 16, 128), F32)
        for x in range(8):
            hot = jnp.where(lo_iota == lo_own[x : x + 1], 1.0, 0.0).astype(BF16)
            match = want == hi_own[x : x + 1]
            for p in range(3):
                rows = [parts[k][p][x : x + 1].astype(F32) for k in range(4)]
                tile = jnp.where(
                    kind == 0, rows[0],
                    jnp.where(kind == 1, rows[1], jnp.where(kind == 2, rows[2], rows[3])),
                )
                lhs = jnp.where(match, jnp.concatenate([tile] * dests, axis=0), 0.0).astype(BF16)
                total = total + lax.dot_general(
                    lhs, hot, (((1,), (1,)), ((), ())), preferred_element_type=F32
                )
        cells[...] = total.reshape(dests, 16, 128)

    finish()
    for g in range(GROUPS):
        copy(g).wait()


def step_two_call(spec, u, v, msq, mask, hq_w, hq_e, rn, rs, owner, weight, dests):
    return pl.pallas_call(
        step_two_kernel,
        in_specs=[SMEM] + [VMEM] * 11,
        out_specs=[HBM, VMEM],
        out_shape=[FIELD, jax.ShapeDtypeStruct((dests, 16, 128), F32)],
        scratch_shapes=[
            pltpu.VMEM((ND, 8, 128), F32),
            pltpu.VMEM((2, 8, 128), F32),
            BUFFER,
            pltpu.SemaphoreType.DMA((GROUPS,)),
        ],
        compiler_params=PARAMS,
        name="step_two",
    )(jnp.asarray(SCAL), spec, u, v, msq, mask, hq_w, hq_e, rn, rs, owner, weight)


def cell_kernel(parts, stress, rough):
    sums = jnp.sum(parts[...], axis=0)
    w, a, bx, by = (sums[4 * k : 4 * k + 4] for k in range(4))
    total_w = jnp.maximum(w, 1.0)
    sx = bx / total_w
    sy = by / total_w
    low = jnp.maximum(a, 1.0)
    r = jnp.sqrt(1.0 + (bx * bx + by * by) / (low * low)) * a / total_w
    for n in range(4):
        at = slice(n * 128, n * 128 + 128)
        stress[0:1, at] = sx[n : n + 1]
        stress[1:2, at] = sy[n : n + 1]
        rough[0:1, at] = r[n : n + 1]


def cell_call(parts):
    return pl.pallas_call(
        cell_kernel,
        out_shape=[jax.ShapeDtypeStruct((2, 512), F32), jax.ShapeDtypeStruct((1, 512), F32)],
        name="cells",
    )(parts)


def body(spectra, sea_mask, atm_wind, wind_row, owner, weight):
    lons = lax.axis_size("lon")
    lats = lax.axis_size("lat")
    eastward = [(i, (i + 1) % lons) for i in range(lons)]
    westward = [(i, (i - 1) % lons) for i in range(lons)]
    northward = [(i, i + 1) for i in range(lats - 1)]
    southward = [(i + 1, i) for i in range(lats - 1)]

    me = lax.axis_index("lon").astype(jnp.int32)
    mine = sector_call(sea_mask, atm_wind, wind_row, lons)
    near_w, near_e, north, south, msq1 = first_call(spectra)
    table = lax.all_to_all(mine, "lon", 0, 0)
    near_w, near_e, table = lax.optimization_barrier((near_w, near_e, table))
    from_west = lax.ppermute(near_e, "lon", eastward)
    from_east = lax.ppermute(near_w, "lon", westward)
    u, v, side, fn, fs = wind_call(
        me.reshape(1), table, wind_row, msq1, sea_mask, north, south
    )
    rn = lax.ppermute(fn, "lat", northward)
    rs = lax.ppermute(fs, "lat", southward)
    energy, msq2, fn2, fs2, to_w, to_e = step_one_call(
        spectra, u, v, msq1, sea_mask, from_west, from_east, side, rn, rs
    )
    from_west = lax.ppermute(to_e, "lon", eastward)
    from_east = lax.ppermute(to_w, "lon", westward)
    rn = lax.ppermute(fn2, "lat", northward)
    rs = lax.ppermute(fs2, "lat", southward)
    energy, cells = step_two_call(
        energy, u, v, msq2, sea_mask, from_west, from_east, rn, rs, owner, weight, lons
    )
    parts = lax.all_to_all(cells, "lon", 0, 0)
    stress, rough = cell_call(parts)
    return energy, stress, rough.reshape(512)


def solution(mesh):
    in_specs = (
        P(None, "lon", "lat"),
        P("lon", "lat"),
        P(None, ("lat", "lon")),
        P("lon", "lat"),
        P("lon", "lat"),
        P("lon", "lat"),
    )
    out_specs = (P(None, "lon", "lat"), P(None, ("lat", "lon")), P(("lat", "lon")))
    return jax.shard_map(body, mesh=mesh, in_specs=in_specs, out_specs=out_specs, check_vma=False)
```

```python
import functools
import math

import jax
import jax.numpy as jnp
import numpy as np
from jax import lax
from jax.experimental import pallas as pl
from jax.experimental.pallas import tpu as pltpu
from jax.sharding import PartitionSpec as P

NF = 50
ND = 36
HALF = 18
QUAD = 9
GROUPS = 10
FG = NF // GROUPS
TILES = 2 * GROUPS
GB = FG * ND
ROWS = NF * HALF
COL = ROWS + 4
F32 = jnp.float32
BF16 = jnp.bfloat16

_f = np.arange(NF, dtype=np.float64)
_freq = 1.07 ** (_f - (NF - 1))
_theta = 2.0 * math.pi * (np.arange(ND) + 0.5) / ND
_cos = np.cos(_theta)
_sin = np.sin(_theta)
_gain = 0.6 * _freq**2
_base = 1.0 - 0.2 * _freq
_cour = 0.7 * (3.0 / 7.0) ** (_f / (NF - 1))
_slope = 250.0 * _freq**4 / ND
_four = 4.0 * _freq
_push = 800.0 * _freq**2 / ND
EASTWARD = list(range(0, 9)) + list(range(27, 36))
WESTWARD = list(range(9, 27))

SCAL = np.zeros((6, 64), np.float32)
for _i, _t in enumerate((_gain, _base, _cour, _slope, _four, _push)):
    SCAL[_i, :NF] = _t
SCAL = SCAL.reshape(-1)


def scal(sm, kind, f):
    return sm[kind * 64 + f]


def place(i, d):
    return i // 3, (i % 3) * ND + 2 * d


def _lane_tables():
    tab = np.zeros((TILES, 8, 128), np.float32)
    tab[:, 1] = 1.0
    for f in range(NF):
        for d in range(HALF):
            h, j = place(f % FG, d)
            values = (_gain[f], _base[f], _cos[d], _sin[d], _four[f], _cour[f])
            for r, value in enumerate(values):
                tab[2 * (f // FG) + h, r, j : j + 2] = value
    return tab


def _dir_tables():
    tab = np.zeros((4, HALF, 128), np.float32)
    for s, dirs in enumerate((EASTWARD, WESTWARD)):
        tab[2 * s] = _cos[dirs][:, None]
        tab[2 * s + 1] = _sin[dirs][:, None]
    return tab


LANE_TAB = _lane_tables()
DIR_TAB = _dir_tables()
FOUR_COL = np.broadcast_to(_four[:, None], (NF, 128)).astype(np.float32)


def quartets():
    for d in range(QUAD):
        yield (d, 17 - d, 18 + d, 35 - d)


def iota(shape, dim):
    return lax.broadcasted_iota(jnp.int32, shape, dim)


def pack_edges(ref, g, lane):
    pair = lane // 2
    packed = [jnp.zeros((8, 128), F32) for _ in range(4)]
    for i in range(FG):
        for d in range(HALF):
            h, j = place(i, d)
            here = pair == j // 2
            e = ref[g * GB + i * ND + d]
            packed[h] = jnp.where(here, pltpu.roll(e, (j + 2) % 128, 1), packed[h])
            e = ref[g * GB + i * ND + HALF + d]
            packed[2 + h] = jnp.where(here, pltpu.roll(e, j, 1) if j else e, packed[2 + h])
    return packed


def first_kernel(spec_hbm, near_w, near_e, north, south, msq, spec, sems):
    lane = iota((8, 128), 1)

    def copy(g):
        at = pl.ds(g * GB, GB)
        return pltpu.make_async_copy(spec_hbm.at[at], spec.at[at], sems.at[g])

    for g in range(GROUPS):
        copy(g).start()
    msq[...] = jnp.zeros_like(msq)

    def group(g, growth):
        copy(g).wait()
        total = jnp.zeros((8, 128), F32)
        for i in range(FG):
            acc = jnp.zeros((8, 128), F32)
            for d in range(ND):
                e = spec[g * GB + i * ND + d]
                acc = acc + e
                if d in WESTWARD:
                    k = pl.ds(g * FG * HALF + i * HALF + WESTWARD.index(d), 1)
                    near_w[k, :] = e[0:1]
                else:
                    k = pl.ds(g * FG * HALF + i * HALF + EASTWARD.index(d), 1)
                    near_e[k, :] = e[7:8]
            total = total + float(_slope[i]) * acc
        msq[...] += growth * total
        north[2 * g], north[2 * g + 1], south[2 * g], south[2 * g + 1] = pack_edges(spec, g, lane)
        return growth * float(_slope[FG] / _slope[0])

    lax.fori_loop(0, GROUPS, group, jnp.float32(1.0))
    q = msq[...]
    for near, x in ((near_w, 0), (near_e, 7)):
        near[ROWS : ROWS + 1, :] = q[x : x + 1]
        near[ROWS + 1 : COL, :] = jnp.zeros((COL - ROWS - 1, 128), F32)


def sector_kernel(mask, winds, wrow, mine):
    for c in range(2):
        for r in range(16):
            mine[0, 16 * c + r : 16 * c + r + 1, :] = winds[c : c + 1, 128 * r : 128 * r + 128]
    mine[0, 32:40, :] = wrow[...].astype(F32)
    mine[0, 40:48, :] = mask[...].astype(F32)
    mine[0, 48:56, :] = jnp.zeros((8, 128), F32)
    rows = mine[0]
    for n in range(1, mine.shape[0]):
        mine[n] = rows


SMEM = pl.BlockSpec(memory_space=pltpu.SMEM)
VMEM = pl.BlockSpec(memory_space=pltpu.VMEM)
HBM = pl.BlockSpec(memory_space=pltpu.HBM)
TILE = jax.ShapeDtypeStruct((8, 128), F32)
FIELD = jax.ShapeDtypeStruct((NF * ND, 8, 128), F32)
STAGE = jax.ShapeDtypeStruct((4 * NF * ND, 8, 128), F32)
BUFFER = pltpu.VMEM((NF * ND, 8, 128), F32)
PARAMS = pltpu.CompilerParams(vmem_limit_bytes=30 * 2**20)
MIDDLE = pltpu.CompilerParams(vmem_limit_bytes=43 * 2**20)
WIDE = pltpu.CompilerParams(vmem_limit_bytes=48 * 2**20)
ALONE = pltpu.CompilerParams(vmem_limit_bytes=54 * 2**20)


def first_call(spectra):
    edge = jax.ShapeDtypeStruct((COL, 128), F32)
    pack = jax.ShapeDtypeStruct((TILES, 8, 128), F32)
    return pl.pallas_call(
        first_kernel,
        in_specs=[HBM],
        out_specs=[VMEM] * 5,
        out_shape=[edge, edge, pack, pack, TILE],
        scratch_shapes=[BUFFER, pltpu.SemaphoreType.DMA((GROUPS,))],
        compiler_params=WIDE,
        name="first",
    )(spectra)


def sector_call(mask, winds, wrow, lons):
    return pl.pallas_call(
        sector_kernel,
        in_specs=[VMEM] * 3,
        out_specs=VMEM,
        out_shape=jax.ShapeDtypeStruct((lons, 56, 128), F32),
        compiler_params=ALONE,
        name="sector",
    )(mask, winds, wrow)


def split3(x):
    a = x.astype(BF16)
    r = x - a.astype(F32)
    b = r.astype(BF16)
    c = (r - b.astype(F32)).astype(BF16)
    return a, b, c


def wind_kernel(
    me_ref, table, wrow, msq, mask, north, south, lane_tab,
    u_ref, v_ref, side_ref, fn, fs,
):
    srcs = table.shape[0]
    me = me_ref[0]
    hi_count = srcs * 16
    west = table.at[(me + srcs - 1) & (srcs - 1)]
    east = table.at[(me + 1) & (srcs - 1)]
    rows = [wrow[x : x + 1, :] for x in range(8)]
    for ref, x in ((west, 7), (east, 0)):
        rows.append(ref[32 + x : 33 + x, :].astype(jnp.int32))
    local = [r & (hi_count * 128 - 1) for r in rows]
    hi_iota = iota((hi_count, 128), 0)
    hots = []
    for r in local:
        hots.append(jnp.where(hi_iota == r // 128, 1.0, 0.0).astype(BF16))
    hot = jnp.concatenate(hots, axis=1)
    tab = jnp.concatenate(
        [table[:, 16 * c : 16 * c + 16].reshape(hi_count, 128) for c in range(2)], axis=1
    )
    got = None
    for part in split3(tab):
        term = lax.dot_general(
            part, hot, (((0,), (0,)), ((), ())), preferred_element_type=F32
        )
        got = term if got is None else got + term
    lo_iota = iota((128, 128), 0)
    us, vs = [], []
    for n, r in enumerate(local):
        pick = lo_iota == (r & 127)
        at = slice(n * 128, n * 128 + 128)
        us.append(jnp.sum(jnp.where(pick, got[0:128, at], 0.0), axis=0, keepdims=True))
        vs.append(jnp.sum(jnp.where(pick, got[128:256, at], 0.0), axis=0, keepdims=True))
    for x in range(8):
        u_ref[x : x + 1, :] = us[x]
        v_ref[x : x + 1, :] = vs[x]
    for n, (ref, x) in enumerate(((west, 7), (east, 0))):
        side_ref[3 * n : 3 * n + 1, :] = us[8 + n]
        side_ref[3 * n + 1 : 3 * n + 2, :] = vs[8 + n]
        side_ref[3 * n + 2 : 3 * n + 3, :] = ref[40 + x : 41 + x, :]
    side_ref[6:8, :] = jnp.zeros((2, 128), F32)

    maskf = mask[...].astype(F32)
    odd = (iota((8, 128), 1) & 1) == 1
    for edge, out, at, sign in ((north, fn, 126, 1.0), (south, fs, 0, -1.0)):
        pick = lambda a: jnp.where(
            odd,
            jnp.broadcast_to(a[:, at + 1 : at + 2], (8, 128)),
            jnp.broadcast_to(a[:, at : at + 1], (8, 128)),
        )
        ue, ve, me_, qe = pick(u_ref[...]), pick(v_ref[...]), pick(maskf), pick(msq[...])
        for n in range(TILES):
            lt = lane_tab[n]
            along = sign * (lt[2:3] * ue + lt[3:4] * ve)
            t = jnp.maximum(lt[0:1] * along + lt[1:2], 1.0)
            out[n * 8 : n * 8 + 8, :] = edge[n] * t * (me_ / (1.0 + lt[4:5] * qe))


def wind_call(me, table, wrow, msq, mask, north, south):
    edge = jax.ShapeDtypeStruct((TILES * 8, 128), F32)
    return pl.pallas_call(
        wind_kernel,
        in_specs=[SMEM] + [VMEM] * 7,
        out_specs=[VMEM] * 5,
        out_shape=[TILE, TILE, TILE, edge, edge],
        compiler_params=PARAMS,
        name="winds",
    )(me, table, wrow, msq, mask, north, south, jnp.asarray(LANE_TAB))


def bin_lane(s, i, row, up):
    north = 2 * (row + (0 if s == 0 else QUAD)) + 1
    south = 2 * (row + (0 if s == 0 else -QUAD))
    return jnp.where(up, north, south) + (i % 3) * ND


def wind_factor(sm, f, along):
    return jnp.maximum(scal(sm, 0, f) * along + scal(sm, 1, f), 1.0)


def put_row(dst_w, dst_e, f, d, e, x_east, x_west):
    if d in WESTWARD:
        dst_w[pl.ds(f * HALF + WESTWARD.index(d), 1), :] = e[x_west : x_west + 1]
    else:
        dst_e[pl.ds(f * HALF + EASTWARD.index(d), 1), :] = e[x_east : x_east + 1]


def along_table(along, u, v):
    for d in range(ND):
        along[d] = float(_cos[d]) * u + float(_sin[d]) * v


def shifted(gv, d, j, lane, halo_n, halo_s):
    xs = pltpu.roll(gv, 7 if d in WESTWARD else 1, 0)
    if d < HALF:
        halo = pltpu.roll(halo_n, 127 - j, 1)
        ys = jnp.where(lane == 0, halo, pltpu.roll(gv, 1, 1))
    else:
        halo = pltpu.roll(halo_s, 127 - j, 1)
        ys = jnp.where(lane == 127, halo, pltpu.roll(gv, 127, 1))
    return xs, ys


def step_one_kernel(
    sm, spec_hbm, u, v, msq, mask, rn, rs, out, msq2, in_w, in_e, to_w, to_e, spec, along, sems
):
    def copy(g):
        at = pl.ds(g * GB, GB)
        return pltpu.make_async_copy(spec_hbm.at[at], spec.at[at], sems.at[g])

    for g in range(GROUPS):
        copy(g).start()
    lane = iota((8, 128), 1)
    maskf = mask[...].astype(F32)
    along_table(along, u[...], v[...])
    msq2[...] = jnp.zeros_like(msq2)
    for col in (in_w, in_e, to_w, to_e):
        col[ROWS:COL, :] = jnp.zeros((COL - ROWS, 128), F32)

    @pl.loop(0, GROUPS)
    def _(g):
        copy(g).wait()
        total = jnp.zeros((8, 128), F32)
        tiles = [pl.ds(pl.multiple_of(g * 16 + 8 * h, 8), 8) for h in range(2)]
        halo_n = [rn[at, :] for at in tiles]
        halo_s = [rs[at, :] for at in tiles]
        for i in range(FG):
            f = g * FG + i
            cr = scal(sm, 2, f)
            fac = maskf / (1.0 + scal(sm, 4, f) * msq[...])
            a = scal(sm, 0, f) * fac
            b = scal(sm, 1, f) * fac
            acc = jnp.zeros((8, 128), F32)
            for quartet in quartets():
                d0 = quartet[0]
                kx = cr * float(abs(_cos[d0]))
                ky = cr * float(abs(_sin[d0]))
                k0 = 1.0 - kx - ky
                for d in quartet:
                    h, j = place(i, d % HALF)
                    gv = spec[f * ND + d] * jnp.maximum(a * along[d] + b, fac)
                    xs, ys = shifted(gv, d, j, lane, halo_n[h], halo_s[h])
                    e = k0 * gv + kx * xs + ky * ys
                    out[f * ND + d] = e
                    acc = acc + e
                    put_row(to_w, to_e, f, d, e, 7, 0)
                    put_row(in_e, in_w, f, d, e, 0, 7)
            total = total + scal(sm, 3, f) * acc
        msq2[...] += total


def step_one_call(spectra, u, v, msq, mask, rn, rs):
    column = jax.ShapeDtypeStruct((COL, 128), F32)
    return pl.pallas_call(
        step_one_kernel,
        in_specs=[SMEM, HBM] + [VMEM] * 6,
        out_specs=[VMEM] * 6,
        out_shape=[FIELD, TILE, column, column, column, column],
        scratch_shapes=[
            BUFFER,
            pltpu.VMEM((ND, 8, 128), F32),
            pltpu.SemaphoreType.DMA((GROUPS,)),
        ],
        compiler_params=MIDDLE,
        name="step_one",
    )(jnp.asarray(SCAL), spectra, u, v, msq, mask, rn, rs)


def mend_one_kernel(
    sm, near_w, near_e, own_w, own_e, in_w, in_e, to_w, to_e, part, msq, u, v, mask, side, fn, fs,
    lane_tab, dir_tab, four,
    msq2, row_w, row_e, col_w, col_e, fn2, fs2, corner_n, corner_s,
):
    row18 = iota((HALF, 128), 0)
    lane18 = iota((HALF, 128), 1)
    up = row18 < QUAD
    maskf = mask[...].astype(F32)
    msq2[...] = part[...]
    acc = {}
    for s, (near, own, src, dst, x, far) in enumerate(
        ((near_w, own_e, in_w, row_w, 0, 7), (near_e, own_w, in_e, row_e, 7, 0))
    ):
        cos = dir_tab[2 * s]
        sin = dir_tab[2 * s + 1]
        acos = jnp.abs(cos)
        u_row, v_row, mask_row = (side[3 * s + r : 3 * s + r + 1, :] for r in range(3))
        along = cos * u_row + sin * v_row
        fac = mask_row / (1.0 + four[...] * near[ROWS : ROWS + 1, :])
        along_own = cos * u[far : far + 1, :] + sin * v[far : far + 1, :]
        fac_own = maskf[far : far + 1] / (1.0 + four[...] * msq[far : far + 1, :])
        steep = jnp.zeros((HALF, 128), F32)
        for f in range(NF):
            at = slice(f * HALF, f * HALF + HALF)
            g1 = near[at, :] * wind_factor(sm, f, along) * fac[f : f + 1]
            ring = own[at, :] * wind_factor(sm, f, along_own) * fac_own[f : f + 1]
            fix = (scal(sm, 2, f) * acos) * (g1 - ring)
            dst[at, :] = src[at, :] + fix
            steep = steep + scal(sm, 3, f) * fix
            i = f % FG
            tile = 2 * (f // FG) + i // 3
            ends = jnp.where(
                up,
                jnp.broadcast_to(g1[:, 127:128], (HALF, 128)),
                jnp.broadcast_to(g1[:, 0:1], (HALF, 128)),
            )
            ends = jnp.where(lane18 == bin_lane(s, i, row18, up), ends, 0.0)
            for key, val in (("n", jnp.where(up, ends, 0.0)), ("s", jnp.where(up, 0.0, ends))):
                have = acc.get((key, tile))
                acc[(key, tile)] = val if have is None else have + val
        dst[ROWS:COL, :] = jnp.zeros((COL - ROWS, 128), F32)
        msq2[x : x + 1, :] = part[x : x + 1, :] + jnp.sum(steep, axis=0, keepdims=True)
    for key, out in (("n", corner_n), ("s", corner_s)):
        for tile in range(TILES):
            out[tile : tile + 1, :] = jnp.sum(acc[(key, tile)], axis=0, keepdims=True)
    msq2[...] = msq2[...] * maskf

    for s, (src, dst, x) in enumerate(((to_e, col_e, 7), (to_w, col_w, 0))):
        along = dir_tab[2 * s] * u[x : x + 1, :] + dir_tab[2 * s + 1] * v[x : x + 1, :]
        fac = maskf[x : x + 1] / (1.0 + four[...] * msq2[x : x + 1, :])
        for f in range(NF):
            at = slice(f * HALF, f * HALF + HALF)
            dst[at, :] = src[at, :] * wind_factor(sm, f, along) * fac[f : f + 1]
        dst[ROWS:COL, :] = jnp.zeros((COL - ROWS, 128), F32)

    sub = iota((8, 128), 0)
    for own, corner, dst, at, sign in ((fn, corner_n, fn2, 127, 1.0), (fs, corner_s, fs2, 0, -1.0)):
        pick = lambda z: jnp.broadcast_to(z[:, at : at + 1], (8, 128))
        ue, ve, me, qe = pick(u[...]), pick(v[...]), pick(maskf), pick(msq2[...])
        for n in range(TILES):
            lt = lane_tab[n]
            cos, sin = sign * lt[2:3], sign * lt[3:4]
            kx = lt[5:6] * jnp.abs(cos)
            ky = lt[5:6] * jnp.abs(sin)
            g1 = own[n * 8 : n * 8 + 8, :]
            row = corner[n : n + 1, :]
            from_w = jnp.where(sub == 0, row, pltpu.roll(g1, 1, 0))
            from_e = jnp.where(sub == 7, row, pltpu.roll(g1, 7, 0))
            xs = jnp.where(cos > 0.0, from_w, from_e)
            ys = pltpu.roll(g1, 1 if at else 127, 1)
            e = (1.0 - kx - ky) * g1 + kx * xs + ky * ys
            t = jnp.maximum(lt[0:1] * (cos * ue + sin * ve) + lt[1:2], 1.0)
            dst[n * 8 : n * 8 + 8, :] = e * t * (me / (1.0 + lt[4:5] * qe))


def mend_one_call(near_w, near_e, own_w, own_e, in_w, in_e, to_w, to_e, part, msq, u, v, mask, side, fn, fs):
    edge = jax.ShapeDtypeStruct((TILES * 8, 128), F32)
    column = jax.ShapeDtypeStruct((COL, 128), F32)
    return pl.pallas_call(
        mend_one_kernel,
        in_specs=[SMEM] + [VMEM] * 19,
        out_specs=[VMEM] * 7,
        out_shape=[TILE, column, column, column, column, edge, edge],
        scratch_shapes=[pltpu.VMEM((24, 128), F32), pltpu.VMEM((24, 128), F32)],
        compiler_params=PARAMS,
        name="mend_one",
    )(
        jnp.asarray(SCAL), near_w, near_e, own_w, own_e, in_w, in_e, to_w, to_e, part, msq, u, v,
        mask, side, fn, fs, jnp.asarray(LANE_TAB), jnp.asarray(DIR_TAB), jnp.asarray(FOUR_COL),
    )


def step_two_kernel(
    sm, spec, row_w, row_e, u, v, msq, mask, rn, rs, out, push, out_w, out_e, along, field, sems
):
    def copy(g):
        at = pl.ds(g * GB, GB)
        return pltpu.make_async_copy(field.at[at], out.at[at], sems.at[g])

    lane = iota((8, 128), 1)
    sub = iota((8, 128), 0)
    maskf = mask[...].astype(F32)
    along_table(along, u[...], v[...])
    push[...] = jnp.zeros_like(push)

    @pl.loop(0, GROUPS)
    def _(g):
        pu = jnp.zeros((8, 128), F32)
        pv = jnp.zeros((8, 128), F32)
        tiles = [pl.ds(pl.multiple_of(g * 16 + 8 * h, 8), 8) for h in range(2)]
        halo_n = [rn[at, :] for at in tiles]
        halo_s = [rs[at, :] for at in tiles]
        for i in range(FG):
            f = g * FG + i
            a, b, cr = scal(sm, 0, f), scal(sm, 1, f), scal(sm, 2, f)
            fac = maskf / (1.0 + scal(sm, 4, f) * msq[...])
            fu = jnp.zeros((8, 128), F32)
            fv = jnp.zeros((8, 128), F32)
            for quartet in quartets():
                d0 = quartet[0]
                kx = cr * float(abs(_cos[d0]))
                ky = cr * float(abs(_sin[d0]))
                k0 = 1.0 - kx - ky
                kxm = kx * maskf
                kym = ky * maskf
                q = []
                for d in quartet:
                    h, j = place(i, d % HALF)
                    t = jnp.maximum(a * along[d] + b, 1.0)
                    e = spec[f * ND + d]
                    if d in WESTWARD:
                        row = row_e[pl.ds(f * HALF + WESTWARD.index(d), 1), :]
                        e = jnp.where(sub == 7, jnp.broadcast_to(row, (8, 128)), e)
                    else:
                        row = row_w[pl.ds(f * HALF + EASTWARD.index(d), 1), :]
                        e = jnp.where(sub == 0, jnp.broadcast_to(row, (8, 128)), e)
                    gv = e * t * fac
                    xs, ys = shifted(gv, d, j, lane, halo_n[h], halo_s[h])
                    e = k0 * gv + kxm * xs + kym * ys
                    field[f * ND + d] = e
                    put_row(out_e, out_w, f, d, e, 0, 7)
                    q.append((t - 1.0) * e)
                lo = q[0] - q[2]
                hi = q[1] - q[3]
                fu = fu + float(_cos[d0]) * (lo - hi)
                fv = fv + float(_sin[d0]) * (lo + hi)
            pu = pu + scal(sm, 5, f) * fu
            pv = pv + scal(sm, 5, f) * fv
        push[0] += pu
        push[1] += pv
        copy(g).start()

    for col in (out_w, out_e):
        col[ROWS:COL, :] = jnp.zeros((COL - ROWS, 128), F32)
    for g in range(GROUPS):
        copy(g).wait()


def step_two_call(spec, row_w, row_e, u, v, msq, mask, rn, rs):
    column = jax.ShapeDtypeStruct((COL, 128), F32)
    return pl.pallas_call(
        step_two_kernel,
        in_specs=[SMEM] + [VMEM] * 9,
        out_specs=[HBM] + [VMEM] * 3,
        out_shape=[STAGE, jax.ShapeDtypeStruct((2, 8, 128), F32), column, column],
        scratch_shapes=[
            pltpu.VMEM((ND, 8, 128), F32),
            BUFFER,
            pltpu.SemaphoreType.DMA((GROUPS,)),
        ],
        compiler_params=PARAMS,
        name="step_two",
    )(jnp.asarray(SCAL), spec, row_w, row_e, u, v, msq, mask, rn, rs)


def mend_two_kernel(
    sm, halo_w, halo_e, sent_w, sent_e, out_w, out_e, push_in, u, v, mask, owner, weight, dir_tab,
    end_w, end_e, cells, push,
):
    maskf = mask[...].astype(F32)
    push[...] = push_in[...]
    for s, (halo, ring, src, dst, x) in enumerate(
        ((halo_w, sent_e, out_w, end_w, 0), (halo_e, sent_w, out_e, end_e, 7))
    ):
        cos = dir_tab[2 * s]
        sin = dir_tab[2 * s + 1]
        along = cos * u[x : x + 1, :] + sin * v[x : x + 1, :]
        weigh = jnp.abs(cos) * maskf[x : x + 1]
        total = jnp.zeros((HALF, 128), F32)
        for f in range(NF):
            at = slice(f * HALF, f * HALF + HALF)
            fix = (scal(sm, 2, f) * weigh) * (halo[at, :] - ring[at, :])
            dst[at, :] = src[at, :] + fix
            total = total + (scal(sm, 5, f) * (wind_factor(sm, f, along) - 1.0)) * fix
        dst[ROWS:COL, :] = jnp.zeros((COL - ROWS, 128), F32)
        for c, part in ((0, cos), (1, sin)):
            push[c, x : x + 1, :] = push_in[c, x : x + 1, :] + jnp.sum(part * total, axis=0, keepdims=True)

    uu, vv = u[...], v[...]
    share = weight[...].astype(F32) * maskf
    tau = 0.02 * (uu * uu + vv * vv) + 0.25
    terms = (share, share * tau, share * push[0], share * push[1])
    parts = [split3(t) for t in terms]
    dests = cells.shape[0]
    own = owner[...] & (dests * 512 - 1)
    hi_own = own // 128
    lo_own = own & 127
    row = iota((dests * 16, 128), 0)
    want = (row // 16) * 4 + row % 4
    lo_iota = iota((128, 128), 0)
    kind = iota((16, 128), 0) // 4
    total = jnp.zeros((dests * 16, 128), F32)
    for x in range(8):
        hot = jnp.where(lo_iota == lo_own[x : x + 1], 1.0, 0.0).astype(BF16)
        match = want == hi_own[x : x + 1]
        for p in range(3):
            rows = [parts[k][p][x : x + 1].astype(F32) for k in range(4)]
            tile = jnp.where(
                kind == 0, rows[0],
                jnp.where(kind == 1, rows[1], jnp.where(kind == 2, rows[2], rows[3])),
            )
            lhs = jnp.where(match, jnp.concatenate([tile] * dests, axis=0), 0.0).astype(BF16)
            total = total + lax.dot_general(
                lhs, hot, (((1,), (1,)), ((), ())), preferred_element_type=F32
            )
    cells[...] = total.reshape(dests, 16, 128)


def mend_two_call(
    halo_w, halo_e, sent_w, sent_e, out_w, out_e, push, u, v, mask, owner, weight, dests
):
    column = jax.ShapeDtypeStruct((COL, 128), F32)
    return pl.pallas_call(
        mend_two_kernel,
        in_specs=[SMEM] + [VMEM] * 13,
        out_specs=[VMEM] * 3,
        out_shape=[column, column, jax.ShapeDtypeStruct((dests, 16, 128), F32)],
        scratch_shapes=[pltpu.VMEM((2, 8, 128), F32)],
        compiler_params=PARAMS,
        name="mend_two",
    )(
        jnp.asarray(SCAL), halo_w, halo_e, sent_w, sent_e, out_w, out_e, push, u, v, mask, owner,
        weight, jnp.asarray(DIR_TAB),
    )


def output_kernel(stage, end_w, end_e, out, field, whole, sems_in, sems):
    sub = iota((8, 128), 0)

    def copy_in(g):
        at = pl.ds(g * GB, GB)
        return pltpu.make_async_copy(stage.at[at], field.at[at], sems_in.at[g])

    def copy(g):
        at = pl.ds(g * GB, GB)
        return pltpu.make_async_copy(whole.at[at], out.at[at], sems.at[g])

    for g in range(GROUPS):
        copy_in(g).start()

    @pl.loop(0, GROUPS)
    def _(g):
        copy_in(g).wait()
        for i in range(FG):
            f = g * FG + i
            for d in range(ND):
                if d in WESTWARD:
                    row = end_e[pl.ds(f * HALF + WESTWARD.index(d), 1), :]
                    x = 7
                else:
                    row = end_w[pl.ds(f * HALF + EASTWARD.index(d), 1), :]
                    x = 0
                whole[f * ND + d] = jnp.where(sub == x, jnp.broadcast_to(row, (8, 128)), field[f * ND + d])
        copy(g).start()

    for g in range(GROUPS):
        copy(g).wait()


def output_call(field, end_w, end_e):
    return pl.pallas_call(
        output_kernel,
        in_specs=[HBM, VMEM, VMEM],
        out_specs=HBM,
        out_shape=FIELD,
        scratch_shapes=[
            BUFFER,
            BUFFER,
            pltpu.SemaphoreType.DMA((GROUPS,)),
            pltpu.SemaphoreType.DMA((GROUPS,)),
        ],
        compiler_params=PARAMS,
        name="output",
    )(field, end_w, end_e)


def cell_kernel(parts, stress, rough):
    sums = jnp.sum(parts[...], axis=0)
    w, a, bx, by = (sums[4 * k : 4 * k + 4] for k in range(4))
    total_w = jnp.maximum(w, 1.0)
    sx = bx / total_w
    sy = by / total_w
    low = jnp.maximum(a, 1.0)
    r = jnp.sqrt(1.0 + (bx * bx + by * by) / (low * low)) * a / total_w
    for n in range(4):
        at = slice(n * 128, n * 128 + 128)
        stress[0:1, at] = sx[n : n + 1]
        stress[1:2, at] = sy[n : n + 1]
        rough[0:1, at] = r[n : n + 1]


def cell_call(parts):
    return pl.pallas_call(
        cell_kernel,
        out_shape=[jax.ShapeDtypeStruct((2, 512), F32), jax.ShapeDtypeStruct((1, 512), F32)],
        name="cells",
    )(parts)


def body(spectra, sea_mask, atm_wind, wind_row, owner, weight):
    lons = lax.axis_size("lon")
    lats = lax.axis_size("lat")
    eastward = [(i, (i + 1) % lons) for i in range(lons)]
    westward = [(i, (i - 1) % lons) for i in range(lons)]
    northward = [(i, i + 1) for i in range(lats - 1)]
    southward = [(i + 1, i) for i in range(lats - 1)]

    me = lax.axis_index("lon").astype(jnp.int32)
    mine = sector_call(sea_mask, atm_wind, wind_row, lons)
    spectra, mine = lax.optimization_barrier((spectra, mine))
    own_w, own_e, north, south, msq1 = first_call(spectra)
    table = lax.all_to_all(mine, "lon", 0, 0)
    near_w = lax.ppermute(own_e, "lon", eastward)
    near_e = lax.ppermute(own_w, "lon", westward)
    u, v, side, fn, fs = wind_call(
        me.reshape(1), table, wind_row, msq1, sea_mask, north, south
    )
    rn = lax.ppermute(fn, "lat", northward)
    rs = lax.ppermute(fs, "lat", southward)
    energy, part, in_w, in_e, to_w, to_e = step_one_call(
        spectra, u, v, msq1, sea_mask, rn, rs
    )
    msq2, row_w, row_e, col_w, col_e, fn2, fs2 = mend_one_call(
        near_w, near_e, own_w, own_e, in_w, in_e, to_w, to_e, part, msq1, u, v, sea_mask, side, fn, fs
    )
    halo_w = lax.ppermute(col_e, "lon", eastward)
    halo_e = lax.ppermute(col_w, "lon", westward)
    rn = lax.ppermute(fn2, "lat", northward)
    rs = lax.ppermute(fs2, "lat", southward)
    field, push, out_w, out_e = step_two_call(energy, row_w, row_e, u, v, msq2, sea_mask, rn, rs)
    end_w, end_e, cells = mend_two_call(
        halo_w, halo_e, col_w, col_e, out_w, out_e, push, u, v, sea_mask, owner, weight, lons
    )
    parts = lax.all_to_all(cells, "lon", 0, 0)
    energy = output_call(field, end_w, end_e)
    stress, rough = cell_call(parts)
    return energy, stress, rough.reshape(512)


def solution(mesh):
    in_specs = (
        P(None, "lon", "lat"),
        P("lon", "lat"),
        P(None, ("lat", "lon")),
        P("lon", "lat"),
        P("lon", "lat"),
        P("lon", "lat"),
    )
    out_specs = (P(None, "lon", "lat"), P(None, ("lat", "lon")), P(("lat", "lon")))
    return jax.shard_map(body, mesh=mesh, in_specs=in_specs, out_specs=out_specs, check_vma=False)
```

```python
import functools
import math

import jax
import jax.numpy as jnp
import numpy as np
from jax import lax
from jax.experimental import pallas as pl
from jax.experimental.pallas import tpu as pltpu
from jax.sharding import PartitionSpec as P

NF = 50
ND = 36
HALF = 18
QUAD = 9
GROUPS = 10
FG = NF // GROUPS
TILES = 2 * GROUPS
GB = FG * ND
ROWS = NF * HALF
COL = ROWS + 4
F32 = jnp.float32
BF16 = jnp.bfloat16

_f = np.arange(NF, dtype=np.float64)
_freq = 1.07 ** (_f - (NF - 1))
_theta = 2.0 * math.pi * (np.arange(ND) + 0.5) / ND
_cos = np.cos(_theta)
_sin = np.sin(_theta)
_gain = 0.6 * _freq**2
_base = 1.0 - 0.2 * _freq
_cour = 0.7 * (3.0 / 7.0) ** (_f / (NF - 1))
_slope = 250.0 * _freq**4 / ND
_four = 4.0 * _freq
_push = 800.0 * _freq**2 / ND
EASTWARD = list(range(0, 9)) + list(range(27, 36))
WESTWARD = list(range(9, 27))

SCAL = np.zeros((6, 64), np.float32)
for _i, _t in enumerate((_gain, _base, _cour, _slope, _four, _push)):
    SCAL[_i, :NF] = _t
SCAL = SCAL.reshape(-1)


def scal(sm, kind, f):
    return sm[kind * 64 + f]


def place(i, d):
    return i // 3, (i % 3) * ND + 2 * d


def _lane_tables():
    tab = np.zeros((TILES, 8, 128), np.float32)
    tab[:, 1] = 1.0
    for f in range(NF):
        for d in range(HALF):
            h, j = place(f % FG, d)
            values = (
                _gain[f], _base[f], _cos[d], _sin[d], _four[f], _cour[f], _slope[f], _push[f]
            )
            for r, value in enumerate(values):
                tab[2 * (f // FG) + h, r, j : j + 2] = value
    return tab


def _dir_tables():
    tab = np.zeros((4, HALF, 128), np.float32)
    for s, dirs in enumerate((EASTWARD, WESTWARD)):
        tab[2 * s] = _cos[dirs][:, None]
        tab[2 * s + 1] = _sin[dirs][:, None]
    return tab


LANE_TAB = _lane_tables()
DIR_TAB = _dir_tables()
FOUR_COL = np.broadcast_to(_four[:, None], (NF, 128)).astype(np.float32)


def quartets():
    for d in range(QUAD):
        yield (d, 17 - d, 18 + d, 35 - d)


def iota(shape, dim):
    return lax.broadcasted_iota(jnp.int32, shape, dim)


def pack_edges(ref, g, lane):
    pair = lane // 2
    packed = [jnp.zeros((8, 128), F32) for _ in range(4)]
    for i in range(FG):
        for d in range(HALF):
            h, j = place(i, d)
            here = pair == j // 2
            e = ref[g * GB + i * ND + d]
            packed[h] = jnp.where(here, pltpu.roll(e, (j + 2) % 128, 1), packed[h])
            e = ref[g * GB + i * ND + HALF + d]
            packed[2 + h] = jnp.where(here, pltpu.roll(e, j, 1) if j else e, packed[2 + h])
    return packed


def first_kernel(spec_hbm, near_w, near_e, north, south, msq, spec, sems):
    lane = iota((8, 128), 1)

    def copy(g):
        at = pl.ds(g * GB, GB)
        return pltpu.make_async_copy(spec_hbm.at[at], spec.at[at], sems.at[g])

    for g in range(GROUPS):
        copy(g).start()
    msq[...] = jnp.zeros_like(msq)

    def group(g, growth):
        copy(g).wait()
        total = jnp.zeros((8, 128), F32)
        for i in range(FG):
            acc = jnp.zeros((8, 128), F32)
            for d in range(ND):
                e = spec[g * GB + i * ND + d]
                acc = acc + e
                if d in WESTWARD:
                    k = pl.ds(g * FG * HALF + i * HALF + WESTWARD.index(d), 1)
                    near_w[k, :] = e[0:1]
                else:
                    k = pl.ds(g * FG * HALF + i * HALF + EASTWARD.index(d), 1)
                    near_e[k, :] = e[7:8]
            total = total + float(_slope[i]) * acc
        msq[...] += growth * total
        north[2 * g], north[2 * g + 1], south[2 * g], south[2 * g + 1] = pack_edges(spec, g, lane)
        return growth * float(_slope[FG] / _slope[0])

    lax.fori_loop(0, GROUPS, group, jnp.float32(1.0))
    q = msq[...]
    for near, x in ((near_w, 0), (near_e, 7)):
        near[ROWS : ROWS + 1, :] = q[x : x + 1]
        near[ROWS + 1 : COL, :] = jnp.zeros((COL - ROWS - 1, 128), F32)


def sector_kernel(mask, winds, wrow, mine):
    for c in range(2):
        for r in range(16):
            mine[0, 16 * c + r : 16 * c + r + 1, :] = winds[c : c + 1, 128 * r : 128 * r + 128]
    mine[0, 32:40, :] = wrow[...].astype(F32)
    mine[0, 40:48, :] = mask[...].astype(F32)
    mine[0, 48:56, :] = jnp.zeros((8, 128), F32)
    rows = mine[0]
    for n in range(1, mine.shape[0]):
        mine[n] = rows


SMEM = pl.BlockSpec(memory_space=pltpu.SMEM)
VMEM = pl.BlockSpec(memory_space=pltpu.VMEM)
HBM = pl.BlockSpec(memory_space=pltpu.HBM)
TILE = jax.ShapeDtypeStruct((8, 128), F32)
FIELD = jax.ShapeDtypeStruct((NF * ND, 8, 128), F32)
STAGE = jax.ShapeDtypeStruct((4 * NF * ND, 8, 128), F32)
BUFFER = pltpu.VMEM((NF * ND, 8, 128), F32)
PARAMS = pltpu.CompilerParams(vmem_limit_bytes=30 * 2**20)
MIDDLE = pltpu.CompilerParams(vmem_limit_bytes=43 * 2**20)
WIDE = pltpu.CompilerParams(vmem_limit_bytes=48 * 2**20)
ALONE = pltpu.CompilerParams(vmem_limit_bytes=54 * 2**20)


def first_call(spectra):
    edge = jax.ShapeDtypeStruct((COL, 128), F32)
    pack = jax.ShapeDtypeStruct((TILES, 8, 128), F32)
    return pl.pallas_call(
        first_kernel,
        in_specs=[HBM],
        out_specs=[VMEM] * 5,
        out_shape=[edge, edge, pack, pack, TILE],
        scratch_shapes=[BUFFER, pltpu.SemaphoreType.DMA((GROUPS,))],
        compiler_params=WIDE,
        name="first",
    )(spectra)


def sector_call(mask, winds, wrow, lons):
    return pl.pallas_call(
        sector_kernel,
        in_specs=[VMEM] * 3,
        out_specs=VMEM,
        out_shape=jax.ShapeDtypeStruct((lons, 56, 128), F32),
        compiler_params=ALONE,
        name="sector",
    )(mask, winds, wrow)


def split3(x):
    a = x.astype(BF16)
    r = x - a.astype(F32)
    b = r.astype(BF16)
    c = (r - b.astype(F32)).astype(BF16)
    return a, b, c


def wind_kernel(
    me_ref, table, wrow, msq, mask, north, south, lane_tab,
    u_ref, v_ref, side_ref, fn, fs,
):
    srcs = table.shape[0]
    me = me_ref[0]
    hi_count = srcs * 16
    west = table.at[(me + srcs - 1) & (srcs - 1)]
    east = table.at[(me + 1) & (srcs - 1)]
    rows = [wrow[x : x + 1, :] for x in range(8)]
    for ref, x in ((west, 7), (east, 0)):
        rows.append(ref[32 + x : 33 + x, :].astype(jnp.int32))
    local = [r & (hi_count * 128 - 1) for r in rows]
    hi_iota = iota((hi_count, 128), 0)
    hots = []
    for r in local:
        hots.append(jnp.where(hi_iota == r // 128, 1.0, 0.0).astype(BF16))
    hot = jnp.concatenate(hots, axis=1)
    tab = jnp.concatenate(
        [table[:, 16 * c : 16 * c + 16].reshape(hi_count, 128) for c in range(2)], axis=1
    )
    got = None
    for part in split3(tab):
        term = lax.dot_general(
            part, hot, (((0,), (0,)), ((), ())), preferred_element_type=F32
        )
        got = term if got is None else got + term
    lo_iota = iota((128, 128), 0)
    us, vs = [], []
    for n, r in enumerate(local):
        pick = lo_iota == (r & 127)
        at = slice(n * 128, n * 128 + 128)
        us.append(jnp.sum(jnp.where(pick, got[0:128, at], 0.0), axis=0, keepdims=True))
        vs.append(jnp.sum(jnp.where(pick, got[128:256, at], 0.0), axis=0, keepdims=True))
    for x in range(8):
        u_ref[x : x + 1, :] = us[x]
        v_ref[x : x + 1, :] = vs[x]
    for n, (ref, x) in enumerate(((west, 7), (east, 0))):
        side_ref[3 * n : 3 * n + 1, :] = us[8 + n]
        side_ref[3 * n + 1 : 3 * n + 2, :] = vs[8 + n]
        side_ref[3 * n + 2 : 3 * n + 3, :] = ref[40 + x : 41 + x, :]
    side_ref[6:8, :] = jnp.zeros((2, 128), F32)

    maskf = mask[...].astype(F32)
    odd = (iota((8, 128), 1) & 1) == 1
    for edge, out, at, sign in ((north, fn, 126, 1.0), (south, fs, 0, -1.0)):
        pick = lambda a: jnp.where(
            odd,
            jnp.broadcast_to(a[:, at + 1 : at + 2], (8, 128)),
            jnp.broadcast_to(a[:, at : at + 1], (8, 128)),
        )
        ue, ve, me_, qe = pick(u_ref[...]), pick(v_ref[...]), pick(maskf), pick(msq[...])
        for n in range(TILES):
            lt = lane_tab[n]
            along = sign * (lt[2:3] * ue + lt[3:4] * ve)
            t = jnp.maximum(lt[0:1] * along + lt[1:2], 1.0)
            out[n * 8 : n * 8 + 8, :] = edge[n] * t * (me_ / (1.0 + lt[4:5] * qe))


def wind_call(me, table, wrow, msq, mask, north, south):
    edge = jax.ShapeDtypeStruct((TILES * 8, 128), F32)
    return pl.pallas_call(
        wind_kernel,
        in_specs=[SMEM] + [VMEM] * 7,
        out_specs=[VMEM] * 5,
        out_shape=[TILE, TILE, TILE, edge, edge],
        compiler_params=PARAMS,
        name="winds",
    )(me, table, wrow, msq, mask, north, south, jnp.asarray(LANE_TAB))


def bin_lane(s, i, row, up):
    north = 2 * (row + (0 if s == 0 else QUAD)) + 1
    south = 2 * (row + (0 if s == 0 else -QUAD))
    return jnp.where(up, north, south) + (i % 3) * ND


def wind_factor(sm, f, along):
    return jnp.maximum(scal(sm, 0, f) * along + scal(sm, 1, f), 1.0)


def put_row(dst_w, dst_e, f, d, e, x_east, x_west):
    if d in WESTWARD:
        dst_w[pl.ds(f * HALF + WESTWARD.index(d), 1), :] = e[x_west : x_west + 1]
    else:
        dst_e[pl.ds(f * HALF + EASTWARD.index(d), 1), :] = e[x_east : x_east + 1]


def along_table(along, u, v):
    for d in range(ND):
        along[d] = float(_cos[d]) * u + float(_sin[d]) * v


def shifted(gv, d):
    return pltpu.roll(gv, 7 if d in WESTWARD else 1, 0), pltpu.roll(gv, 1 if d < HALF else 127, 1)


def lane_patch(tiles_n, tiles_s, i, d, lane):
    h, j = place(i, d % HALF)
    tile, at = (tiles_n[h], 0) if d < HALF else (tiles_s[h], 127)
    return jnp.where(lane == at, pltpu.roll(tile, 127 - j, 1), 0.0)


def group_tiles(ref, g):
    return [ref[pl.ds(pl.multiple_of(g * 16 + 8 * h, 8), 8), :] for h in range(2)]


def step_one_kernel(
    sm, spec_hbm, u, v, msq, mask, out, msq2, in_w, in_e, to_w, to_e, spec, along, sems
):
    def copy(g):
        at = pl.ds(g * GB, GB)
        return pltpu.make_async_copy(spec_hbm.at[at], spec.at[at], sems.at[g])

    for g in range(GROUPS):
        copy(g).start()
    maskf = mask[...].astype(F32)
    along_table(along, u[...], v[...])
    msq2[...] = jnp.zeros_like(msq2)
    for col in (in_w, in_e, to_w, to_e):
        col[ROWS:COL, :] = jnp.zeros((COL - ROWS, 128), F32)

    @pl.loop(0, GROUPS)
    def _(g):
        copy(g).wait()
        total = jnp.zeros((8, 128), F32)
        for i in range(FG):
            f = g * FG + i
            cr = scal(sm, 2, f)
            fac = maskf / (1.0 + scal(sm, 4, f) * msq[...])
            a = scal(sm, 0, f) * fac
            b = scal(sm, 1, f) * fac
            acc = jnp.zeros((8, 128), F32)
            for quartet in quartets():
                d0 = quartet[0]
                kx = cr * float(abs(_cos[d0]))
                ky = cr * float(abs(_sin[d0]))
                k0 = 1.0 - kx - ky
                for d in quartet:
                    gv = spec[f * ND + d] * jnp.maximum(a * along[d] + b, fac)
                    xs, ys = shifted(gv, d)
                    e = k0 * gv + kx * xs + ky * ys
                    out[f * ND + d] = e
                    acc = acc + e
                    put_row(to_w, to_e, f, d, e, 7, 0)
                    put_row(in_e, in_w, f, d, e, 0, 7)
            total = total + scal(sm, 3, f) * acc
        msq2[...] += total


def step_one_call(spectra, u, v, msq, mask):
    column = jax.ShapeDtypeStruct((COL, 128), F32)
    return pl.pallas_call(
        step_one_kernel,
        in_specs=[SMEM, HBM] + [VMEM] * 4,
        out_specs=[VMEM] * 6,
        out_shape=[FIELD, TILE, column, column, column, column],
        scratch_shapes=[
            BUFFER,
            pltpu.VMEM((ND, 8, 128), F32),
            pltpu.SemaphoreType.DMA((GROUPS,)),
        ],
        compiler_params=MIDDLE,
        name="step_one",
    )(jnp.asarray(SCAL), spectra, u, v, msq, mask)


def mend_one_kernel(
    sm, near_w, near_e, own_w, own_e, in_w, in_e, to_w, to_e, part, msq, u, v, mask, side, fn, fs,
    rn, rs, lane_tab, dir_tab, four,
    msq2, row_w, row_e, col_w, col_e, fn2, fs2, patch_n, patch_s, corner_n, corner_s,
):
    row18 = iota((HALF, 128), 0)
    lane18 = iota((HALF, 128), 1)
    up = row18 < QUAD
    maskf = mask[...].astype(F32)
    msq2[...] = part[...]
    acc = {}
    for s, (near, own, src, dst, x, far) in enumerate(
        ((near_w, own_e, in_w, row_w, 0, 7), (near_e, own_w, in_e, row_e, 7, 0))
    ):
        cos = dir_tab[2 * s]
        sin = dir_tab[2 * s + 1]
        acos = jnp.abs(cos)
        u_row, v_row, mask_row = (side[3 * s + r : 3 * s + r + 1, :] for r in range(3))
        along = cos * u_row + sin * v_row
        fac = mask_row / (1.0 + four[...] * near[ROWS : ROWS + 1, :])
        along_own = cos * u[far : far + 1, :] + sin * v[far : far + 1, :]
        fac_own = maskf[far : far + 1] / (1.0 + four[...] * msq[far : far + 1, :])
        steep = jnp.zeros((HALF, 128), F32)
        for f in range(NF):
            at = slice(f * HALF, f * HALF + HALF)
            g1 = near[at, :] * wind_factor(sm, f, along) * fac[f : f + 1]
            ring = own[at, :] * wind_factor(sm, f, along_own) * fac_own[f : f + 1]
            fix = (scal(sm, 2, f) * acos) * (g1 - ring)
            dst[at, :] = src[at, :] + fix
            steep = steep + scal(sm, 3, f) * fix
            i = f % FG
            tile = 2 * (f // FG) + i // 3
            ends = jnp.where(
                up,
                jnp.broadcast_to(g1[:, 127:128], (HALF, 128)),
                jnp.broadcast_to(g1[:, 0:1], (HALF, 128)),
            )
            ends = jnp.where(lane18 == bin_lane(s, i, row18, up), ends, 0.0)
            for key, val in (("n", jnp.where(up, ends, 0.0)), ("s", jnp.where(up, 0.0, ends))):
                have = acc.get((key, tile))
                acc[(key, tile)] = val if have is None else have + val
        dst[ROWS:COL, :] = jnp.zeros((COL - ROWS, 128), F32)
        msq2[x : x + 1, :] = part[x : x + 1, :] + jnp.sum(steep, axis=0, keepdims=True)
    for key, out in (("n", corner_n), ("s", corner_s)):
        for tile in range(TILES):
            out[tile : tile + 1, :] = jnp.sum(acc[(key, tile)], axis=0, keepdims=True)
    lane = iota((8, 128), 1)
    for own, halo, dst, odd, at in ((fn, rn, patch_n, 1, 0), (fs, rs, patch_s, 0, 127)):
        steep = jnp.zeros((8, 128), F32)
        for n in range(TILES):
            lt = lane_tab[n]
            rows = slice(n * 8, n * 8 + 8)
            fix = lt[5:6] * jnp.abs(lt[3:4]) * (halo[rows, :] - own[rows, :])
            dst[rows, :] = fix
            steep = steep + lt[6:7] * fix
        steep = jnp.sum(jnp.where((lane & 1) == odd, steep, 0.0), axis=1, keepdims=True)
        msq2[...] += jnp.where(lane == at, steep, 0.0)
    msq2[...] = msq2[...] * maskf

    end = lane18 == jnp.where(up, 0, 127)
    for s, (src, dst, x) in enumerate(((to_e, col_e, 7), (to_w, col_w, 0))):
        along = dir_tab[2 * s] * u[x : x + 1, :] + dir_tab[2 * s + 1] * v[x : x + 1, :]
        fac = maskf[x : x + 1] / (1.0 + four[...] * msq2[x : x + 1, :])
        for f in range(NF):
            at = slice(f * HALF, f * HALF + HALF)
            i = f % FG
            row = (2 * (f // FG) + i // 3) * 8 + x
            fix = jnp.where(up, patch_n[row : row + 1, :], patch_s[row : row + 1, :])
            fix = jnp.where(lane18 == bin_lane(s, i, row18, up), fix, 0.0)
            e = src[at, :] + jnp.where(end, jnp.sum(fix, axis=1, keepdims=True), 0.0)
            dst[at, :] = e * wind_factor(sm, f, along) * fac[f : f + 1]
        dst[ROWS:COL, :] = jnp.zeros((COL - ROWS, 128), F32)

    sub = iota((8, 128), 0)
    for own, corner, dst, at, sign in ((fn, corner_n, fn2, 127, 1.0), (fs, corner_s, fs2, 0, -1.0)):
        pick = lambda z: jnp.broadcast_to(z[:, at : at + 1], (8, 128))
        ue, ve, me, qe = pick(u[...]), pick(v[...]), pick(maskf), pick(msq2[...])
        for n in range(TILES):
            lt = lane_tab[n]
            cos, sin = sign * lt[2:3], sign * lt[3:4]
            kx = lt[5:6] * jnp.abs(cos)
            ky = lt[5:6] * jnp.abs(sin)
            g1 = own[n * 8 : n * 8 + 8, :]
            row = corner[n : n + 1, :]
            from_w = jnp.where(sub == 0, row, pltpu.roll(g1, 1, 0))
            from_e = jnp.where(sub == 7, row, pltpu.roll(g1, 7, 0))
            xs = jnp.where(cos > 0.0, from_w, from_e)
            ys = pltpu.roll(g1, 1 if at else 127, 1)
            e = (1.0 - kx - ky) * g1 + kx * xs + ky * ys
            t = jnp.maximum(lt[0:1] * (cos * ue + sin * ve) + lt[1:2], 1.0)
            dst[n * 8 : n * 8 + 8, :] = e * t * (me / (1.0 + lt[4:5] * qe))


def mend_one_call(near_w, near_e, own_w, own_e, in_w, in_e, to_w, to_e, part, msq, u, v, mask, side, fn, fs, rn, rs):
    edge = jax.ShapeDtypeStruct((TILES * 8, 128), F32)
    column = jax.ShapeDtypeStruct((COL, 128), F32)
    return pl.pallas_call(
        mend_one_kernel,
        in_specs=[SMEM] + [VMEM] * 21,
        out_specs=[VMEM] * 9,
        out_shape=[TILE, column, column, column, column, edge, edge, edge, edge],
        scratch_shapes=[pltpu.VMEM((24, 128), F32), pltpu.VMEM((24, 128), F32)],
        compiler_params=PARAMS,
        name="mend_one",
    )(
        jnp.asarray(SCAL), near_w, near_e, own_w, own_e, in_w, in_e, to_w, to_e, part, msq, u, v,
        mask, side, fn, fs, rn, rs, jnp.asarray(LANE_TAB), jnp.asarray(DIR_TAB), jnp.asarray(FOUR_COL),
    )


def step_two_kernel(
    sm, spec, row_w, row_e, u, v, msq, mask, patch_n, patch_s, out, push, out_w, out_e, along, field, sems
):
    def copy(g):
        at = pl.ds(g * GB, GB)
        return pltpu.make_async_copy(field.at[at], out.at[at], sems.at[g])

    lane = iota((8, 128), 1)
    sub = iota((8, 128), 0)
    maskf = mask[...].astype(F32)
    along_table(along, u[...], v[...])
    push[...] = jnp.zeros_like(push)

    @pl.loop(0, GROUPS)
    def _(g):
        pu = jnp.zeros((8, 128), F32)
        pv = jnp.zeros((8, 128), F32)
        tiles_n = group_tiles(patch_n, g)
        tiles_s = group_tiles(patch_s, g)
        for i in range(FG):
            f = g * FG + i
            a, b, cr = scal(sm, 0, f), scal(sm, 1, f), scal(sm, 2, f)
            fac = maskf / (1.0 + scal(sm, 4, f) * msq[...])
            fu = jnp.zeros((8, 128), F32)
            fv = jnp.zeros((8, 128), F32)
            for quartet in quartets():
                d0 = quartet[0]
                kx = cr * float(abs(_cos[d0]))
                ky = cr * float(abs(_sin[d0]))
                k0 = 1.0 - kx - ky
                kxm = kx * maskf
                kym = ky * maskf
                q = []
                for d in quartet:
                    t = jnp.maximum(a * along[d] + b, 1.0)
                    e = spec[f * ND + d]
                    if d in WESTWARD:
                        row = row_e[pl.ds(f * HALF + WESTWARD.index(d), 1), :]
                        e = jnp.where(sub == 7, jnp.broadcast_to(row, (8, 128)), e)
                    else:
                        row = row_w[pl.ds(f * HALF + EASTWARD.index(d), 1), :]
                        e = jnp.where(sub == 0, jnp.broadcast_to(row, (8, 128)), e)
                    e = e + lane_patch(tiles_n, tiles_s, i, d, lane)
                    gv = e * t * fac
                    xs, ys = shifted(gv, d)
                    e = k0 * gv + kxm * xs + kym * ys
                    field[f * ND + d] = e
                    put_row(out_e, out_w, f, d, e, 0, 7)
                    q.append((t - 1.0) * e)
                lo = q[0] - q[2]
                hi = q[1] - q[3]
                fu = fu + float(_cos[d0]) * (lo - hi)
                fv = fv + float(_sin[d0]) * (lo + hi)
            pu = pu + scal(sm, 5, f) * fu
            pv = pv + scal(sm, 5, f) * fv
        push[0] += pu
        push[1] += pv
        copy(g).start()

    for col in (out_w, out_e):
        col[ROWS:COL, :] = jnp.zeros((COL - ROWS, 128), F32)
    for g in range(GROUPS):
        copy(g).wait()


def step_two_call(spec, row_w, row_e, u, v, msq, mask, patch_n, patch_s):
    column = jax.ShapeDtypeStruct((COL, 128), F32)
    return pl.pallas_call(
        step_two_kernel,
        in_specs=[SMEM] + [VMEM] * 9,
        out_specs=[HBM] + [VMEM] * 3,
        out_shape=[STAGE, jax.ShapeDtypeStruct((2, 8, 128), F32), column, column],
        scratch_shapes=[
            pltpu.VMEM((ND, 8, 128), F32),
            BUFFER,
            pltpu.SemaphoreType.DMA((GROUPS,)),
        ],
        compiler_params=PARAMS,
        name="step_two",
    )(jnp.asarray(SCAL), spec, row_w, row_e, u, v, msq, mask, patch_n, patch_s)


def mend_two_kernel(
    sm, halo_w, halo_e, sent_w, sent_e, out_w, out_e, push_in, u, v, mask, owner, weight,
    own_n, own_s, rn, rs, lane_tab, dir_tab,
    end_w, end_e, cells, patch_n, patch_s, push,
):
    maskf = mask[...].astype(F32)
    push[...] = push_in[...]
    for s, (halo, ring, src, dst, x) in enumerate(
        ((halo_w, sent_e, out_w, end_w, 0), (halo_e, sent_w, out_e, end_e, 7))
    ):
        cos = dir_tab[2 * s]
        sin = dir_tab[2 * s + 1]
        along = cos * u[x : x + 1, :] + sin * v[x : x + 1, :]
        weigh = jnp.abs(cos) * maskf[x : x + 1]
        total = jnp.zeros((HALF, 128), F32)
        for f in range(NF):
            at = slice(f * HALF, f * HALF + HALF)
            fix = (scal(sm, 2, f) * weigh) * (halo[at, :] - ring[at, :])
            dst[at, :] = src[at, :] + fix
            total = total + (scal(sm, 5, f) * (wind_factor(sm, f, along) - 1.0)) * fix
        dst[ROWS:COL, :] = jnp.zeros((COL - ROWS, 128), F32)
        for c, part in ((0, cos), (1, sin)):
            push[c, x : x + 1, :] = push_in[c, x : x + 1, :] + jnp.sum(part * total, axis=0, keepdims=True)
    lane = iota((8, 128), 1)
    for own, halo, dst, odd, at, sign in (
        (own_n, rn, patch_n, 1, 0, 1.0), (own_s, rs, patch_s, 0, 127, -1.0)
    ):
        pick = lambda z: jnp.broadcast_to(z[:, at : at + 1], (8, 128))
        ue, ve, me = pick(u[...]), pick(v[...]), pick(maskf)
        tu = jnp.zeros((8, 128), F32)
        tv = jnp.zeros((8, 128), F32)
        for n in range(TILES):
            lt = lane_tab[n]
            rows = slice(n * 8, n * 8 + 8)
            cos, sin = sign * lt[2:3], sign * lt[3:4]
            fix = lt[5:6] * jnp.abs(sin) * me * (halo[rows, :] - own[rows, :])
            dst[rows, :] = fix
            rate = jnp.maximum(lt[0:1] * (cos * ue + sin * ve) + lt[1:2], 1.0) - 1.0
            q = lt[7:8] * rate * fix
            tu = tu + cos * q
            tv = tv + sin * q
        for c, part in ((0, tu), (1, tv)):
            part = jnp.sum(jnp.where((lane & 1) == odd, part, 0.0), axis=1, keepdims=True)
            push[c] += jnp.where(lane == at, part, 0.0)

    uu, vv = u[...], v[...]
    share = weight[...].astype(F32) * maskf
    tau = 0.02 * (uu * uu + vv * vv) + 0.25
    terms = (share, share * tau, share * push[0], share * push[1])
    parts = [split3(t) for t in terms]
    dests = cells.shape[0]
    own = owner[...] & (dests * 512 - 1)
    hi_own = own // 128
    lo_own = own & 127
    row = iota((dests * 16, 128), 0)
    want = (row // 16) * 4 + row % 4
    lo_iota = iota((128, 128), 0)
    kind = iota((16, 128), 0) // 4
    total = jnp.zeros((dests * 16, 128), F32)
    for x in range(8):
        hot = jnp.where(lo_iota == lo_own[x : x + 1], 1.0, 0.0).astype(BF16)
        match = want == hi_own[x : x + 1]
        for p in range(3):
            rows = [parts[k][p][x : x + 1].astype(F32) for k in range(4)]
            tile = jnp.where(
                kind == 0, rows[0],
                jnp.where(kind == 1, rows[1], jnp.where(kind == 2, rows[2], rows[3])),
            )
            lhs = jnp.where(match, jnp.concatenate([tile] * dests, axis=0), 0.0).astype(BF16)
            total = total + lax.dot_general(
                lhs, hot, (((1,), (1,)), ((), ())), preferred_element_type=F32
            )
    cells[...] = total.reshape(dests, 16, 128)


def mend_two_call(
    halo_w, halo_e, sent_w, sent_e, out_w, out_e, push, u, v, mask, owner, weight,
    own_n, own_s, rn, rs, dests,
):
    edge = jax.ShapeDtypeStruct((TILES * 8, 128), F32)
    column = jax.ShapeDtypeStruct((COL, 128), F32)
    return pl.pallas_call(
        mend_two_kernel,
        in_specs=[SMEM] + [VMEM] * 18,
        out_specs=[VMEM] * 5,
        out_shape=[column, column, jax.ShapeDtypeStruct((dests, 16, 128), F32), edge, edge],
        scratch_shapes=[pltpu.VMEM((2, 8, 128), F32)],
        compiler_params=PARAMS,
        name="mend_two",
    )(
        jnp.asarray(SCAL), halo_w, halo_e, sent_w, sent_e, out_w, out_e, push, u, v, mask, owner,
        weight, own_n, own_s, rn, rs, jnp.asarray(LANE_TAB), jnp.asarray(DIR_TAB),
    )


def output_kernel(stage, end_w, end_e, patch_n, patch_s, out, field, whole, sems_in, sems):
    sub = iota((8, 128), 0)
    lane = iota((8, 128), 1)

    def copy_in(g):
        at = pl.ds(g * GB, GB)
        return pltpu.make_async_copy(stage.at[at], field.at[at], sems_in.at[g])

    def copy(g):
        at = pl.ds(g * GB, GB)
        return pltpu.make_async_copy(whole.at[at], out.at[at], sems.at[g])

    for g in range(GROUPS):
        copy_in(g).start()

    @pl.loop(0, GROUPS)
    def _(g):
        copy_in(g).wait()
        tiles_n = group_tiles(patch_n, g)
        tiles_s = group_tiles(patch_s, g)
        for i in range(FG):
            f = g * FG + i
            for d in range(ND):
                if d in WESTWARD:
                    row = end_e[pl.ds(f * HALF + WESTWARD.index(d), 1), :]
                    x = 7
                else:
                    row = end_w[pl.ds(f * HALF + EASTWARD.index(d), 1), :]
                    x = 0
                e = jnp.where(sub == x, jnp.broadcast_to(row, (8, 128)), field[f * ND + d])
                whole[f * ND + d] = e + lane_patch(tiles_n, tiles_s, i, d, lane)
        copy(g).start()

    for g in range(GROUPS):
        copy(g).wait()


def output_call(field, end_w, end_e, patch_n, patch_s):
    return pl.pallas_call(
        output_kernel,
        in_specs=[HBM] + [VMEM] * 4,
        out_specs=HBM,
        out_shape=FIELD,
        scratch_shapes=[
            BUFFER,
            BUFFER,
            pltpu.SemaphoreType.DMA((GROUPS,)),
            pltpu.SemaphoreType.DMA((GROUPS,)),
        ],
        compiler_params=PARAMS,
        name="output",
    )(field, end_w, end_e, patch_n, patch_s)


def cell_kernel(parts, stress, rough):
    sums = jnp.sum(parts[...], axis=0)
    w, a, bx, by = (sums[4 * k : 4 * k + 4] for k in range(4))
    total_w = jnp.maximum(w, 1.0)
    sx = bx / total_w
    sy = by / total_w
    low = jnp.maximum(a, 1.0)
    r = jnp.sqrt(1.0 + (bx * bx + by * by) / (low * low)) * a / total_w
    for n in range(4):
        at = slice(n * 128, n * 128 + 128)
        stress[0:1, at] = sx[n : n + 1]
        stress[1:2, at] = sy[n : n + 1]
        rough[0:1, at] = r[n : n + 1]


def cell_call(parts):
    return pl.pallas_call(
        cell_kernel,
        out_shape=[jax.ShapeDtypeStruct((2, 512), F32), jax.ShapeDtypeStruct((1, 512), F32)],
        name="cells",
    )(parts)


def body(spectra, sea_mask, atm_wind, wind_row, owner, weight):
    lons = lax.axis_size("lon")
    lats = lax.axis_size("lat")
    eastward = [(i, (i + 1) % lons) for i in range(lons)]
    westward = [(i, (i - 1) % lons) for i in range(lons)]
    northward = [(i, i + 1) for i in range(lats - 1)]
    southward = [(i + 1, i) for i in range(lats - 1)]

    me = lax.axis_index("lon").astype(jnp.int32)
    mine = sector_call(sea_mask, atm_wind, wind_row, lons)
    spectra, mine = lax.optimization_barrier((spectra, mine))
    own_w, own_e, north, south, msq1 = first_call(spectra)
    table = lax.all_to_all(mine, "lon", 0, 0)
    near_w = lax.ppermute(own_e, "lon", eastward)
    near_e = lax.ppermute(own_w, "lon", westward)
    u, v, side, fn, fs = wind_call(
        me.reshape(1), table, wind_row, msq1, sea_mask, north, south
    )
    rn = lax.ppermute(fn, "lat", northward)
    rs = lax.ppermute(fs, "lat", southward)
    energy, part, in_w, in_e, to_w, to_e = step_one_call(
        spectra, u, v, msq1, sea_mask
    )
    msq2, row_w, row_e, col_w, col_e, fn2, fs2, patch_n, patch_s = mend_one_call(
        near_w, near_e, own_w, own_e, in_w, in_e, to_w, to_e, part, msq1, u, v, sea_mask, side,
        fn, fs, rn, rs,
    )
    halo_w = lax.ppermute(col_e, "lon", eastward)
    halo_e = lax.ppermute(col_w, "lon", westward)
    rn = lax.ppermute(fn2, "lat", northward)
    rs = lax.ppermute(fs2, "lat", southward)
    field, push, out_w, out_e = step_two_call(
        energy, row_w, row_e, u, v, msq2, sea_mask, patch_n, patch_s
    )
    end_w, end_e, cells, patch_n, patch_s = mend_two_call(
        halo_w, halo_e, col_w, col_e, out_w, out_e, push, u, v, sea_mask, owner, weight,
        fn2, fs2, rn, rs, lons,
    )
    parts = lax.all_to_all(cells, "lon", 0, 0)
    energy = output_call(field, end_w, end_e, patch_n, patch_s)
    stress, rough = cell_call(parts)
    return energy, stress, rough.reshape(512)


def solution(mesh):
    in_specs = (
        P(None, "lon", "lat"),
        P("lon", "lat"),
        P(None, ("lat", "lon")),
        P("lon", "lat"),
        P("lon", "lat"),
        P("lon", "lat"),
    )
    out_specs = (P(None, "lon", "lat"), P(None, ("lat", "lon")), P(("lat", "lon")))
    return jax.shard_map(body, mesh=mesh, in_specs=in_specs, out_specs=out_specs, check_vma=False)
```

```python
import functools
import math

import jax
import jax.numpy as jnp
import numpy as np
from jax import lax
from jax.experimental import pallas as pl
from jax.experimental.pallas import tpu as pltpu
from jax.sharding import PartitionSpec as P

NF = 50
ND = 36
HALF = 18
QUAD = 9
GROUPS = 10
FG = NF // GROUPS
TILES = 2 * GROUPS
GB = FG * ND
ROWS = NF * HALF
COL = ROWS + 4
F32 = jnp.float32
BF16 = jnp.bfloat16

_f = np.arange(NF, dtype=np.float64)
_freq = 1.07 ** (_f - (NF - 1))
_theta = 2.0 * math.pi * (np.arange(ND) + 0.5) / ND
_cos = np.cos(_theta)
_sin = np.sin(_theta)
_gain = 0.6 * _freq**2
_base = 1.0 - 0.2 * _freq
_cour = 0.7 * (3.0 / 7.0) ** (_f / (NF - 1))
_slope = 250.0 * _freq**4 / ND
_four = 4.0 * _freq
_push = 800.0 * _freq**2 / ND
EASTWARD = list(range(0, 9)) + list(range(27, 36))
WESTWARD = list(range(9, 27))

SCAL = np.zeros((6, 64), np.float32)
for _i, _t in enumerate((_gain, _base, _cour, _slope, _four, _push)):
    SCAL[_i, :NF] = _t
SCAL = SCAL.reshape(-1)


def scal(sm, kind, f):
    return sm[kind * 64 + f]


def place(i, d):
    return i // 3, (i % 3) * ND + 2 * d


def _lane_tables():
    tab = np.zeros((TILES, 8, 128), np.float32)
    tab[:, 1] = 1.0
    for f in range(NF):
        for d in range(HALF):
            h, j = place(f % FG, d)
            values = (
                _gain[f], _base[f], _cos[d], _sin[d], _four[f], _cour[f], _slope[f], _push[f]
            )
            for r, value in enumerate(values):
                tab[2 * (f // FG) + h, r, j : j + 2] = value
    return tab


def _dir_tables():
    tab = np.zeros((4, HALF, 128), np.float32)
    for s, dirs in enumerate((EASTWARD, WESTWARD)):
        tab[2 * s] = _cos[dirs][:, None]
        tab[2 * s + 1] = _sin[dirs][:, None]
    return tab


LANE_TAB = _lane_tables()
DIR_TAB = _dir_tables()
FOUR_COL = np.broadcast_to(_four[:, None], (NF, 128)).astype(np.float32)


def quartets():
    for d in range(QUAD):
        yield (d, 17 - d, 18 + d, 35 - d)


def iota(shape, dim):
    return lax.broadcasted_iota(jnp.int32, shape, dim)


def pack_edges(ref, g, lane):
    pair = lane // 2
    packed = [jnp.zeros((8, 128), F32) for _ in range(4)]
    for i in range(FG):
        for d in range(HALF):
            h, j = place(i, d)
            here = pair == j // 2
            e = ref[g * GB + i * ND + d]
            packed[h] = jnp.where(here, pltpu.roll(e, (j + 2) % 128, 1), packed[h])
            e = ref[g * GB + i * ND + HALF + d]
            packed[2 + h] = jnp.where(here, pltpu.roll(e, j, 1) if j else e, packed[2 + h])
    return packed


def first_kernel(uneven, spec_hbm, near_w, near_e, send_a, send_b, north, south, msq, spec, sems):
    lane = iota((8, 128), 1)

    def copy(g):
        at = pl.ds(g * GB, GB)
        return pltpu.make_async_copy(spec_hbm.at[at], spec.at[at], sems.at[g])

    for g in range(GROUPS):
        copy(g).start()
    msq[...] = jnp.zeros_like(msq)

    def group(g, growth):
        copy(g).wait()
        total = jnp.zeros((8, 128), F32)
        for i in range(FG):
            acc = jnp.zeros((8, 128), F32)
            for d in range(ND):
                e = spec[g * GB + i * ND + d]
                acc = acc + e
                if d in WESTWARD:
                    k = pl.ds(g * FG * HALF + i * HALF + WESTWARD.index(d), 1)
                    near_w[k, :] = e[0:1]
                else:
                    k = pl.ds(g * FG * HALF + i * HALF + EASTWARD.index(d), 1)
                    near_e[k, :] = e[7:8]
            total = total + float(_slope[i]) * acc
        msq[...] += growth * total
        north[2 * g], north[2 * g + 1], south[2 * g], south[2 * g + 1] = pack_edges(spec, g, lane)
        return growth * float(_slope[FG] / _slope[0])

    lax.fori_loop(0, GROUPS, group, jnp.float32(1.0))
    q = msq[...]
    for near, x in ((near_w, 0), (near_e, 7)):
        near[ROWS : ROWS + 1, :] = q[x : x + 1]
        near[ROWS + 1 : COL, :] = jnp.zeros((COL - ROWS - 1, 128), F32)
    east, west = near_e[...], near_w[...]
    send_a[...] = jnp.where(uneven[0] == 1, west, east)
    send_b[...] = jnp.where(uneven[0] == 1, east, west)


def sector_kernel(mask, winds, wrow, mine):
    for c in range(2):
        for r in range(16):
            mine[0, 16 * c + r : 16 * c + r + 1, :] = winds[c : c + 1, 128 * r : 128 * r + 128]
    mine[0, 32:40, :] = wrow[...].astype(F32)
    mine[0, 40:48, :] = mask[...].astype(F32)
    mine[0, 48:56, :] = jnp.zeros((8, 128), F32)
    rows = mine[0]
    for n in range(1, mine.shape[0]):
        mine[n] = rows


SMEM = pl.BlockSpec(memory_space=pltpu.SMEM)
VMEM = pl.BlockSpec(memory_space=pltpu.VMEM)
HBM = pl.BlockSpec(memory_space=pltpu.HBM)
TILE = jax.ShapeDtypeStruct((8, 128), F32)
FIELD = jax.ShapeDtypeStruct((NF * ND, 8, 128), F32)
STAGE = jax.ShapeDtypeStruct((4 * NF * ND, 8, 128), F32)
BUFFER = pltpu.VMEM((NF * ND, 8, 128), F32)
PARAMS = pltpu.CompilerParams(vmem_limit_bytes=30 * 2**20)
MIDDLE = pltpu.CompilerParams(vmem_limit_bytes=43 * 2**20)
WIDE = pltpu.CompilerParams(vmem_limit_bytes=48 * 2**20)
ALONE = pltpu.CompilerParams(vmem_limit_bytes=54 * 2**20)


def first_call(uneven, spectra):
    edge = jax.ShapeDtypeStruct((COL, 128), F32)
    pack = jax.ShapeDtypeStruct((TILES, 8, 128), F32)
    return pl.pallas_call(
        first_kernel,
        in_specs=[SMEM, HBM],
        out_specs=[VMEM] * 7,
        out_shape=[edge, edge, edge, edge, pack, pack, TILE],
        scratch_shapes=[BUFFER, pltpu.SemaphoreType.DMA((GROUPS,))],
        compiler_params=WIDE,
        name="first",
    )(uneven, spectra)


def sector_call(mask, winds, wrow, lons):
    return pl.pallas_call(
        sector_kernel,
        in_specs=[VMEM] * 3,
        out_specs=VMEM,
        out_shape=jax.ShapeDtypeStruct((lons, 56, 128), F32),
        compiler_params=ALONE,
        name="sector",
    )(mask, winds, wrow)


def split3(x):
    a = x.astype(BF16)
    r = x - a.astype(F32)
    b = r.astype(BF16)
    c = (r - b.astype(F32)).astype(BF16)
    return a, b, c


def wind_kernel(
    me_ref, table, wrow, msq, mask, north, south, lane_tab,
    u_ref, v_ref, side_ref, fn, fs,
):
    srcs = table.shape[0]
    me = me_ref[0]
    hi_count = srcs * 16
    west = table.at[(me + srcs - 1) & (srcs - 1)]
    east = table.at[(me + 1) & (srcs - 1)]
    rows = [wrow[x : x + 1, :] for x in range(8)]
    for ref, x in ((west, 7), (east, 0)):
        rows.append(ref[32 + x : 33 + x, :].astype(jnp.int32))
    local = [r & (hi_count * 128 - 1) for r in rows]
    hi_iota = iota((hi_count, 128), 0)
    hots = []
    for r in local:
        hots.append(jnp.where(hi_iota == r // 128, 1.0, 0.0).astype(BF16))
    hot = jnp.concatenate(hots, axis=1)
    tab = jnp.concatenate(
        [table[:, 16 * c : 16 * c + 16].reshape(hi_count, 128) for c in range(2)], axis=1
    )
    got = None
    for part in split3(tab):
        term = lax.dot_general(
            part, hot, (((0,), (0,)), ((), ())), preferred_element_type=F32
        )
        got = term if got is None else got + term
    lo_iota = iota((128, 128), 0)
    us, vs = [], []
    for n, r in enumerate(local):
        pick = lo_iota == (r & 127)
        at = slice(n * 128, n * 128 + 128)
        us.append(jnp.sum(jnp.where(pick, got[0:128, at], 0.0), axis=0, keepdims=True))
        vs.append(jnp.sum(jnp.where(pick, got[128:256, at], 0.0), axis=0, keepdims=True))
    for x in range(8):
        u_ref[x : x + 1, :] = us[x]
        v_ref[x : x + 1, :] = vs[x]
    for n, (ref, x) in enumerate(((west, 7), (east, 0))):
        side_ref[3 * n : 3 * n + 1, :] = us[8 + n]
        side_ref[3 * n + 1 : 3 * n + 2, :] = vs[8 + n]
        side_ref[3 * n + 2 : 3 * n + 3, :] = ref[40 + x : 41 + x, :]
    side_ref[6:8, :] = jnp.zeros((2, 128), F32)

    maskf = mask[...].astype(F32)
    odd = (iota((8, 128), 1) & 1) == 1
    for edge, out, at, sign in ((north, fn, 126, 1.0), (south, fs, 0, -1.0)):
        pick = lambda a: jnp.where(
            odd,
            jnp.broadcast_to(a[:, at + 1 : at + 2], (8, 128)),
            jnp.broadcast_to(a[:, at : at + 1], (8, 128)),
        )
        ue, ve, me_, qe = pick(u_ref[...]), pick(v_ref[...]), pick(maskf), pick(msq[...])
        for n in range(TILES):
            lt = lane_tab[n]
            along = sign * (lt[2:3] * ue + lt[3:4] * ve)
            t = jnp.maximum(lt[0:1] * along + lt[1:2], 1.0)
            out[n * 8 : n * 8 + 8, :] = edge[n] * t * (me_ / (1.0 + lt[4:5] * qe))


def wind_call(me, table, wrow, msq, mask, north, south):
    edge = jax.ShapeDtypeStruct((TILES * 8, 128), F32)
    return pl.pallas_call(
        wind_kernel,
        in_specs=[SMEM] + [VMEM] * 7,
        out_specs=[VMEM] * 5,
        out_shape=[TILE, TILE, TILE, edge, edge],
        compiler_params=PARAMS,
        name="winds",
    )(me, table, wrow, msq, mask, north, south, jnp.asarray(LANE_TAB))


def bin_lane(s, i, row, up):
    north = 2 * (row + (0 if s == 0 else QUAD)) + 1
    south = 2 * (row + (0 if s == 0 else -QUAD))
    return jnp.where(up, north, south) + (i % 3) * ND


def wind_factor(sm, f, along):
    return jnp.maximum(scal(sm, 0, f) * along + scal(sm, 1, f), 1.0)


def put_row(dst_w, dst_e, f, d, e, x_east, x_west):
    if d in WESTWARD:
        dst_w[pl.ds(f * HALF + WESTWARD.index(d), 1), :] = e[x_west : x_west + 1]
    else:
        dst_e[pl.ds(f * HALF + EASTWARD.index(d), 1), :] = e[x_east : x_east + 1]


def along_table(along, u, v):
    for d in range(ND):
        along[d] = float(_cos[d]) * u + float(_sin[d]) * v


def shifted(gv, d):
    return pltpu.roll(gv, 7 if d in WESTWARD else 1, 0), pltpu.roll(gv, 1 if d < HALF else 127, 1)


def lane_patch(tiles_n, tiles_s, i, d, lane):
    h, j = place(i, d % HALF)
    tile, at = (tiles_n[h], 0) if d < HALF else (tiles_s[h], 127)
    return jnp.where(lane == at, pltpu.roll(tile, 127 - j, 1), 0.0)


def group_tiles(ref, g):
    return [ref[pl.ds(pl.multiple_of(g * 16 + 8 * h, 8), 8), :] for h in range(2)]


def step_one_kernel(
    sm, spec_hbm, u, v, msq, mask, out, msq2, in_w, in_e, to_w, to_e, spec, along, sems
):
    def copy(g):
        at = pl.ds(g * GB, GB)
        return pltpu.make_async_copy(spec_hbm.at[at], spec.at[at], sems.at[g])

    for g in range(GROUPS):
        copy(g).start()
    maskf = mask[...].astype(F32)
    along_table(along, u[...], v[...])
    msq2[...] = jnp.zeros_like(msq2)
    for col in (in_w, in_e, to_w, to_e):
        col[ROWS:COL, :] = jnp.zeros((COL - ROWS, 128), F32)

    @pl.loop(0, GROUPS)
    def _(g):
        copy(g).wait()
        total = jnp.zeros((8, 128), F32)
        for i in range(FG):
            f = g * FG + i
            cr = scal(sm, 2, f)
            fac = maskf / (1.0 + scal(sm, 4, f) * msq[...])
            a = scal(sm, 0, f) * fac
            b = scal(sm, 1, f) * fac
            acc = jnp.zeros((8, 128), F32)
            for quartet in quartets():
                d0 = quartet[0]
                kx = cr * float(abs(_cos[d0]))
                ky = cr * float(abs(_sin[d0]))
                k0 = 1.0 - kx - ky
                for d in quartet:
                    gv = spec[f * ND + d] * jnp.maximum(a * along[d] + b, fac)
                    xs, ys = shifted(gv, d)
                    e = k0 * gv + kx * xs + ky * ys
                    out[f * ND + d] = e
                    acc = acc + e
                    put_row(to_w, to_e, f, d, e, 7, 0)
                    put_row(in_e, in_w, f, d, e, 0, 7)
            total = total + scal(sm, 3, f) * acc
        msq2[...] += total


def step_one_call(spectra, u, v, msq, mask):
    column = jax.ShapeDtypeStruct((COL, 128), F32)
    return pl.pallas_call(
        step_one_kernel,
        in_specs=[SMEM, HBM] + [VMEM] * 4,
        out_specs=[VMEM] * 6,
        out_shape=[FIELD, TILE, column, column, column, column],
        scratch_shapes=[
            BUFFER,
            pltpu.VMEM((ND, 8, 128), F32),
            pltpu.SemaphoreType.DMA((GROUPS,)),
        ],
        compiler_params=MIDDLE,
        name="step_one",
    )(jnp.asarray(SCAL), spectra, u, v, msq, mask)


def mend_one_kernel(
    sm, near_w, near_e, own_w, own_e, in_w, in_e, to_w, to_e, part, msq, u, v, mask, side, fn, fs,
    rn, rs, lane_tab, dir_tab, four,
    msq2, row_w, row_e, col_w, col_e, fn2, fs2, patch_n, patch_s, corner,
):
    row18 = iota((HALF, 128), 0)
    lane18 = iota((HALF, 128), 1)
    up = row18 < QUAD
    maskf = mask[...].astype(F32)
    msq2[...] = part[...]
    acc = {}
    for s, (near, own, src, dst, x, far) in enumerate(
        ((near_w, own_e, in_w, row_w, 0, 7), (near_e, own_w, in_e, row_e, 7, 0))
    ):
        cos = dir_tab[2 * s]
        sin = dir_tab[2 * s + 1]
        acos = jnp.abs(cos)
        u_row, v_row, mask_row = (side[3 * s + r : 3 * s + r + 1, :] for r in range(3))
        along = cos * u_row + sin * v_row
        fac = mask_row / (1.0 + four[...] * near[ROWS : ROWS + 1, :])
        along_own = cos * u[far : far + 1, :] + sin * v[far : far + 1, :]
        fac_own = maskf[far : far + 1] / (1.0 + four[...] * msq[far : far + 1, :])
        steep = jnp.zeros((HALF, 128), F32)
        for f in range(NF):
            at = slice(f * HALF, f * HALF + HALF)
            g1 = near[at, :] * wind_factor(sm, f, along) * fac[f : f + 1]
            ring = own[at, :] * wind_factor(sm, f, along_own) * fac_own[f : f + 1]
            fix = (scal(sm, 2, f) * acos) * (g1 - ring)
            dst[at, :] = src[at, :] + fix
            steep = steep + scal(sm, 3, f) * fix
            i = f % FG
            tile = 2 * (f // FG) + i // 3
            ends = jnp.where(
                up,
                jnp.broadcast_to(g1[:, 127:128], (HALF, 128)),
                jnp.broadcast_to(g1[:, 0:1], (HALF, 128)),
            )
            ends = jnp.where(lane18 == bin_lane(s, i, row18, up), ends, 0.0)
            acc[tile] = acc[tile] + ends if tile in acc else ends
        dst[ROWS:COL, :] = jnp.zeros((COL - ROWS, 128), F32)
        msq2[x : x + 1, :] = part[x : x + 1, :] + jnp.sum(steep, axis=0, keepdims=True)
    for tile in range(TILES):
        corner[tile : tile + 1, :] = jnp.sum(acc[tile], axis=0, keepdims=True)

    lane = iota((8, 128), 1)
    for own, halo, dst, odd, at in ((fn, rn, patch_n, 1, 0), (fs, rs, patch_s, 0, 127)):
        steep = jnp.zeros((8, 128), F32)
        for n in range(TILES):
            lt = lane_tab[n]
            rows = slice(n * 8, n * 8 + 8)
            fix = lt[5:6] * jnp.abs(lt[3:4]) * (halo[rows, :] - own[rows, :])
            dst[rows, :] = fix
            steep = steep + lt[6:7] * fix
        steep = jnp.sum(jnp.where((lane & 1) == odd, steep, 0.0), axis=1, keepdims=True)
        msq2[...] += jnp.where(lane == at, steep, 0.0)
    msq2[...] = msq2[...] * maskf

    end = lane18 == jnp.where(up, 0, 127)
    for s, (src, dst, x) in enumerate(((to_e, col_e, 7), (to_w, col_w, 0))):
        along = dir_tab[2 * s] * u[x : x + 1, :] + dir_tab[2 * s + 1] * v[x : x + 1, :]
        fac = maskf[x : x + 1] / (1.0 + four[...] * msq2[x : x + 1, :])
        for f in range(NF):
            at = slice(f * HALF, f * HALF + HALF)
            i = f % FG
            row = (2 * (f // FG) + i // 3) * 8 + x
            fix = jnp.where(up, patch_n[row : row + 1, :], patch_s[row : row + 1, :])
            fix = jnp.where(lane18 == bin_lane(s, i, row18, up), fix, 0.0)
            e = src[at, :] + jnp.where(end, jnp.sum(fix, axis=1, keepdims=True), 0.0)
            dst[at, :] = e * wind_factor(sm, f, along) * fac[f : f + 1]
        dst[ROWS:COL, :] = jnp.zeros((COL - ROWS, 128), F32)

    sub = iota((8, 128), 0)
    for own, dst, at, sign in ((fn, fn2, 127, 1.0), (fs, fs2, 0, -1.0)):
        pick = lambda z: jnp.broadcast_to(z[:, at : at + 1], (8, 128))
        ue, ve, me, qe = pick(u[...]), pick(v[...]), pick(maskf), pick(msq2[...])
        for n in range(TILES):
            lt = lane_tab[n]
            cos, sin = sign * lt[2:3], sign * lt[3:4]
            kx = lt[5:6] * jnp.abs(cos)
            ky = lt[5:6] * jnp.abs(sin)
            g1 = own[n * 8 : n * 8 + 8, :]
            row = corner[n : n + 1, :]
            from_w = jnp.where(sub == 0, row, pltpu.roll(g1, 1, 0))
            from_e = jnp.where(sub == 7, row, pltpu.roll(g1, 7, 0))
            xs = jnp.where(cos > 0.0, from_w, from_e)
            ys = pltpu.roll(g1, 1 if at else 127, 1)
            e = (1.0 - kx - ky) * g1 + kx * xs + ky * ys
            t = jnp.maximum(lt[0:1] * (cos * ue + sin * ve) + lt[1:2], 1.0)
            dst[n * 8 : n * 8 + 8, :] = e * t * (me / (1.0 + lt[4:5] * qe))


def mend_one_call(near_w, near_e, own_w, own_e, in_w, in_e, to_w, to_e, part, msq, u, v, mask, side, fn, fs, rn, rs):
    edge = jax.ShapeDtypeStruct((TILES * 8, 128), F32)
    column = jax.ShapeDtypeStruct((COL, 128), F32)
    return pl.pallas_call(
        mend_one_kernel,
        in_specs=[SMEM] + [VMEM] * 21,
        out_specs=[VMEM] * 9,
        out_shape=[TILE, column, column, column, column, edge, edge, edge, edge],
        scratch_shapes=[pltpu.VMEM((24, 128), F32)],
        compiler_params=PARAMS,
        name="mend_one",
    )(
        jnp.asarray(SCAL), near_w, near_e, own_w, own_e, in_w, in_e, to_w, to_e, part, msq, u, v,
        mask, side, fn, fs, rn, rs, jnp.asarray(LANE_TAB), jnp.asarray(DIR_TAB), jnp.asarray(FOUR_COL),
    )


def step_two_kernel(
    sm, spec, row_w, row_e, u, v, msq, mask, patch_n, patch_s, out, push, out_w, out_e, along, field, sems
):
    def copy(g):
        at = pl.ds(g * GB, GB)
        return pltpu.make_async_copy(field.at[at], out.at[at], sems.at[g])

    lane = iota((8, 128), 1)
    sub = iota((8, 128), 0)
    maskf = mask[...].astype(F32)
    along_table(along, u[...], v[...])
    push[...] = jnp.zeros_like(push)

    @pl.loop(0, GROUPS)
    def _(g):
        pu = jnp.zeros((8, 128), F32)
        pv = jnp.zeros((8, 128), F32)
        tiles_n = group_tiles(patch_n, g)
        tiles_s = group_tiles(patch_s, g)
        for i in range(FG):
            f = g * FG + i
            a, b, cr = scal(sm, 0, f), scal(sm, 1, f), scal(sm, 2, f)
            fac = maskf / (1.0 + scal(sm, 4, f) * msq[...])
            fu = jnp.zeros((8, 128), F32)
            fv = jnp.zeros((8, 128), F32)
            for quartet in quartets():
                d0 = quartet[0]
                kx = cr * float(abs(_cos[d0]))
                ky = cr * float(abs(_sin[d0]))
                k0 = 1.0 - kx - ky
                kxm = kx * maskf
                kym = ky * maskf
                q = []
                for d in quartet:
                    t = jnp.maximum(a * along[d] + b, 1.0)
                    e = spec[f * ND + d]
                    if d in WESTWARD:
                        row = row_e[pl.ds(f * HALF + WESTWARD.index(d), 1), :]
                        e = jnp.where(sub == 7, jnp.broadcast_to(row, (8, 128)), e)
                    else:
                        row = row_w[pl.ds(f * HALF + EASTWARD.index(d), 1), :]
                        e = jnp.where(sub == 0, jnp.broadcast_to(row, (8, 128)), e)
                    e = e + lane_patch(tiles_n, tiles_s, i, d, lane)
                    gv = e * t * fac
                    xs, ys = shifted(gv, d)
                    e = k0 * gv + kxm * xs + kym * ys
                    field[f * ND + d] = e
                    put_row(out_e, out_w, f, d, e, 0, 7)
                    q.append((t - 1.0) * e)
                lo = q[0] - q[2]
                hi = q[1] - q[3]
                fu = fu + float(_cos[d0]) * (lo - hi)
                fv = fv + float(_sin[d0]) * (lo + hi)
            pu = pu + scal(sm, 5, f) * fu
            pv = pv + scal(sm, 5, f) * fv
        push[0] += pu
        push[1] += pv
        copy(g).start()

    for col in (out_w, out_e):
        col[ROWS:COL, :] = jnp.zeros((COL - ROWS, 128), F32)
    for g in range(GROUPS):
        copy(g).wait()


def step_two_call(spec, row_w, row_e, u, v, msq, mask, patch_n, patch_s):
    column = jax.ShapeDtypeStruct((COL, 128), F32)
    return pl.pallas_call(
        step_two_kernel,
        in_specs=[SMEM] + [VMEM] * 9,
        out_specs=[HBM] + [VMEM] * 3,
        out_shape=[STAGE, jax.ShapeDtypeStruct((2, 8, 128), F32), column, column],
        scratch_shapes=[
            pltpu.VMEM((ND, 8, 128), F32),
            BUFFER,
            pltpu.SemaphoreType.DMA((GROUPS,)),
        ],
        compiler_params=PARAMS,
        name="step_two",
    )(jnp.asarray(SCAL), spec, row_w, row_e, u, v, msq, mask, patch_n, patch_s)


def mend_two_kernel(
    sm, halo_w, halo_e, sent_w, sent_e, out_w, out_e, push_in, u, v, mask, owner, weight,
    own_n, own_s, rn, rs, lane_tab, dir_tab,
    end_w, end_e, cells, patch_n, patch_s, push,
):
    maskf = mask[...].astype(F32)
    push[...] = push_in[...]
    for s, (halo, ring, src, dst, x) in enumerate(
        ((halo_w, sent_e, out_w, end_w, 0), (halo_e, sent_w, out_e, end_e, 7))
    ):
        cos = dir_tab[2 * s]
        sin = dir_tab[2 * s + 1]
        along = cos * u[x : x + 1, :] + sin * v[x : x + 1, :]
        weigh = jnp.abs(cos) * maskf[x : x + 1]
        total = jnp.zeros((HALF, 128), F32)
        for f in range(NF):
            at = slice(f * HALF, f * HALF + HALF)
            fix = (scal(sm, 2, f) * weigh) * (halo[at, :] - ring[at, :])
            dst[at, :] = src[at, :] + fix
            total = total + (scal(sm, 5, f) * (wind_factor(sm, f, along) - 1.0)) * fix
        dst[ROWS:COL, :] = jnp.zeros((COL - ROWS, 128), F32)
        for c, part in ((0, cos), (1, sin)):
            push[c, x : x + 1, :] = push_in[c, x : x + 1, :] + jnp.sum(part * total, axis=0, keepdims=True)
    lane = iota((8, 128), 1)
    for own, halo, dst, odd, at, sign in (
        (own_n, rn, patch_n, 1, 0, 1.0), (own_s, rs, patch_s, 0, 127, -1.0)
    ):
        pick = lambda z: jnp.broadcast_to(z[:, at : at + 1], (8, 128))
        ue, ve, me = pick(u[...]), pick(v[...]), pick(maskf)
        tu = jnp.zeros((8, 128), F32)
        tv = jnp.zeros((8, 128), F32)
        for n in range(TILES):
            lt = lane_tab[n]
            rows = slice(n * 8, n * 8 + 8)
            cos, sin = sign * lt[2:3], sign * lt[3:4]
            fix = lt[5:6] * jnp.abs(sin) * me * (halo[rows, :] - own[rows, :])
            dst[rows, :] = fix
            rate = jnp.maximum(lt[0:1] * (cos * ue + sin * ve) + lt[1:2], 1.0) - 1.0
            q = lt[7:8] * rate * fix
            tu = tu + cos * q
            tv = tv + sin * q
        for c, part in ((0, tu), (1, tv)):
            part = jnp.sum(jnp.where((lane & 1) == odd, part, 0.0), axis=1, keepdims=True)
            push[c] += jnp.where(lane == at, part, 0.0)

    uu, vv = u[...], v[...]
    share = weight[...].astype(F32) * maskf
    tau = 0.02 * (uu * uu + vv * vv) + 0.25
    terms = (share, share * tau, share * push[0], share * push[1])
    parts = [split3(t) for t in terms]
    dests = cells.shape[0]
    own = owner[...] & (dests * 512 - 1)
    hi_own = own // 128
    lo_own = own & 127
    row = iota((dests * 16, 128), 0)
    want = (row // 16) * 4 + row % 4
    lo_iota = iota((128, 128), 0)
    kind = iota((16, 128), 0) // 4
    total = jnp.zeros((dests * 16, 128), F32)
    for x in range(8):
        hot = jnp.where(lo_iota == lo_own[x : x + 1], 1.0, 0.0).astype(BF16)
        match = want == hi_own[x : x + 1]
        for p in range(3):
            rows = [parts[k][p][x : x + 1].astype(F32) for k in range(4)]
            tile = jnp.where(
                kind == 0, rows[0],
                jnp.where(kind == 1, rows[1], jnp.where(kind == 2, rows[2], rows[3])),
            )
            lhs = jnp.where(match, jnp.concatenate([tile] * dests, axis=0), 0.0).astype(BF16)
            total = total + lax.dot_general(
                lhs, hot, (((1,), (1,)), ((), ())), preferred_element_type=F32
            )
    cells[...] = total.reshape(dests, 16, 128)


def mend_two_call(
    halo_w, halo_e, sent_w, sent_e, out_w, out_e, push, u, v, mask, owner, weight,
    own_n, own_s, rn, rs, dests,
):
    edge = jax.ShapeDtypeStruct((TILES * 8, 128), F32)
    column = jax.ShapeDtypeStruct((COL, 128), F32)
    return pl.pallas_call(
        mend_two_kernel,
        in_specs=[SMEM] + [VMEM] * 18,
        out_specs=[VMEM] * 5,
        out_shape=[column, column, jax.ShapeDtypeStruct((dests, 16, 128), F32), edge, edge],
        scratch_shapes=[pltpu.VMEM((2, 8, 128), F32)],
        compiler_params=PARAMS,
        name="mend_two",
    )(
        jnp.asarray(SCAL), halo_w, halo_e, sent_w, sent_e, out_w, out_e, push, u, v, mask, owner,
        weight, own_n, own_s, rn, rs, jnp.asarray(LANE_TAB), jnp.asarray(DIR_TAB),
    )


def output_kernel(stage, end_w, end_e, patch_n, patch_s, out, field, whole, sems_in, sems):
    sub = iota((8, 128), 0)
    lane = iota((8, 128), 1)

    def copy_in(g):
        at = pl.ds(g * GB, GB)
        return pltpu.make_async_copy(stage.at[at], field.at[at], sems_in.at[g])

    def copy(g):
        at = pl.ds(g * GB, GB)
        return pltpu.make_async_copy(whole.at[at], out.at[at], sems.at[g])

    for g in range(GROUPS):
        copy_in(g).start()

    @pl.loop(0, GROUPS)
    def _(g):
        copy_in(g).wait()
        tiles_n = group_tiles(patch_n, g)
        tiles_s = group_tiles(patch_s, g)
        for i in range(FG):
            f = g * FG + i
            for d in range(ND):
                if d in WESTWARD:
                    row = end_e[pl.ds(f * HALF + WESTWARD.index(d), 1), :]
                    x = 7
                else:
                    row = end_w[pl.ds(f * HALF + EASTWARD.index(d), 1), :]
                    x = 0
                e = jnp.where(sub == x, jnp.broadcast_to(row, (8, 128)), field[f * ND + d])
                whole[f * ND + d] = e + lane_patch(tiles_n, tiles_s, i, d, lane)
        copy(g).start()

    for g in range(GROUPS):
        copy(g).wait()


def output_call(field, end_w, end_e, patch_n, patch_s):
    return pl.pallas_call(
        output_kernel,
        in_specs=[HBM] + [VMEM] * 4,
        out_specs=HBM,
        out_shape=FIELD,
        scratch_shapes=[
            BUFFER,
            BUFFER,
            pltpu.SemaphoreType.DMA((GROUPS,)),
            pltpu.SemaphoreType.DMA((GROUPS,)),
        ],
        compiler_params=PARAMS,
        name="output",
    )(field, end_w, end_e, patch_n, patch_s)


def cell_kernel(parts, stress, rough):
    sums = jnp.sum(parts[...], axis=0)
    w, a, bx, by = (sums[4 * k : 4 * k + 4] for k in range(4))
    total_w = jnp.maximum(w, 1.0)
    sx = bx / total_w
    sy = by / total_w
    low = jnp.maximum(a, 1.0)
    r = jnp.sqrt(1.0 + (bx * bx + by * by) / (low * low)) * a / total_w
    for n in range(4):
        at = slice(n * 128, n * 128 + 128)
        stress[0:1, at] = sx[n : n + 1]
        stress[1:2, at] = sy[n : n + 1]
        rough[0:1, at] = r[n : n + 1]


def cell_call(parts):
    return pl.pallas_call(
        cell_kernel,
        out_shape=[jax.ShapeDtypeStruct((2, 512), F32), jax.ShapeDtypeStruct((1, 512), F32)],
        compiler_params=ALONE,
        name="cells",
    )(parts)


def body(spectra, sea_mask, atm_wind, wind_row, owner, weight):
    lons = lax.axis_size("lon")
    lats = lax.axis_size("lat")
    me = lax.axis_index("lon").astype(jnp.int32)
    odd = (lax.axis_index("lat") & 1) == 1
    uneven = (lax.axis_index("lon") & 1) == 1
    pairs = [(i, i ^ 1) for i in range(lons)]
    others = [(i, (i + 1 if i & 1 else i - 1) % lons) for i in range(lons)]

    def arrive(send_a, send_b):
        first = lax.ppermute(send_a, "lon", pairs)
        second = lax.ppermute(send_b, "lon", others)
        return jnp.where(uneven, first, second), jnp.where(uneven, second, first)

    def trade(east, west):
        return arrive(jnp.where(uneven, west, east), jnp.where(uneven, east, west))

    inside = [(i, i ^ 1) for i in range(lats)]
    across = [(i, i + 1 if i & 1 else i - 1) for i in range(1, lats - 1)]

    def swap(north, south):
        first = lax.ppermute(jnp.where(odd, south, north), "lat", inside)
        second = lax.ppermute(jnp.where(odd, north, south), "lat", across)
        return jnp.where(odd, first, second), jnp.where(odd, second, first)

    mine = sector_call(sea_mask, atm_wind, wind_row, lons)
    spectra, mine = lax.optimization_barrier((spectra, mine))
    own_w, own_e, send_a, send_b, north, south, msq1 = first_call((me & 1).reshape(1), spectra)
    table = lax.all_to_all(mine, "lon", 0, 0)
    near_w, near_e = arrive(send_a, send_b)
    u, v, side, fn, fs = wind_call(
        me.reshape(1), table, wind_row, msq1, sea_mask, north, south
    )
    rn, rs = swap(fn, fs)
    energy, part, in_w, in_e, to_w, to_e = step_one_call(
        spectra, u, v, msq1, sea_mask
    )
    msq2, row_w, row_e, col_w, col_e, fn2, fs2, patch_n, patch_s = mend_one_call(
        near_w, near_e, own_w, own_e, in_w, in_e, to_w, to_e, part, msq1, u, v, sea_mask, side,
        fn, fs, rn, rs,
    )
    halo_w, halo_e = trade(col_e, col_w)
    rn, rs = swap(fn2, fs2)
    field, push, out_w, out_e = step_two_call(
        energy, row_w, row_e, u, v, msq2, sea_mask, patch_n, patch_s
    )
    end_w, end_e, cells, patch_n, patch_s = mend_two_call(
        halo_w, halo_e, col_w, col_e, out_w, out_e, push, u, v, sea_mask, owner, weight,
        fn2, fs2, rn, rs, lons,
    )
    parts = lax.all_to_all(cells, "lon", 0, 0)
    energy = output_call(field, end_w, end_e, patch_n, patch_s)
    stress, rough = cell_call(parts)
    return energy, stress, rough.reshape(512)


def solution(mesh):
    in_specs = (
        P(None, "lon", "lat"),
        P("lon", "lat"),
        P(None, ("lat", "lon")),
        P("lon", "lat"),
        P("lon", "lat"),
        P("lon", "lat"),
    )
    out_specs = (P(None, "lon", "lat"), P(None, ("lat", "lon")), P(("lat", "lon")))
    return jax.shard_map(body, mesh=mesh, in_specs=in_specs, out_specs=out_specs, check_vma=False)
```

```python
import functools
import math

import jax
import jax.numpy as jnp
import numpy as np
from jax import lax
from jax.experimental import pallas as pl
from jax.experimental.pallas import tpu as pltpu
from jax.sharding import PartitionSpec as P

NF = 50
ND = 36
HALF = 18
QUAD = 9
GROUPS = 10
FG = NF // GROUPS
TILES = 2 * GROUPS
GB = FG * ND
ROWS = NF * HALF
COL = ROWS + 4
F32 = jnp.float32
BF16 = jnp.bfloat16

_f = np.arange(NF, dtype=np.float64)
_freq = 1.07 ** (_f - (NF - 1))
_theta = 2.0 * math.pi * (np.arange(ND) + 0.5) / ND
_cos = np.cos(_theta)
_sin = np.sin(_theta)
_gain = 0.6 * _freq**2
_base = 1.0 - 0.2 * _freq
_cour = 0.7 * (3.0 / 7.0) ** (_f / (NF - 1))
_slope = 250.0 * _freq**4 / ND
_four = 4.0 * _freq
_push = 800.0 * _freq**2 / ND
EASTWARD = list(range(0, 9)) + list(range(27, 36))
WESTWARD = list(range(9, 27))

SCAL = np.zeros((6, 64), np.float32)
for _i, _t in enumerate((_gain, _base, _cour, _slope, _four, _push)):
    SCAL[_i, :NF] = _t
SCAL = SCAL.reshape(-1)


def scal(sm, kind, f):
    return sm[kind * 64 + f]


def place(i, d):
    return i // 3, (i % 3) * ND + 2 * d


def _lane_tables():
    tab = np.zeros((TILES, 8, 128), np.float32)
    tab[:, 1] = 1.0
    for f in range(NF):
        for d in range(HALF):
            h, j = place(f % FG, d)
            values = (
                _gain[f], _base[f], _cos[d], _sin[d], _four[f], _cour[f], _slope[f], _push[f]
            )
            for r, value in enumerate(values):
                tab[2 * (f // FG) + h, r, j : j + 2] = value
    return tab


def _dir_tables():
    tab = np.zeros((4, HALF, 128), np.float32)
    for s, dirs in enumerate((EASTWARD, WESTWARD)):
        tab[2 * s] = _cos[dirs][:, None]
        tab[2 * s + 1] = _sin[dirs][:, None]
    return tab


LANE_TAB = _lane_tables()
DIR_TAB = _dir_tables()
FOUR_COL = np.broadcast_to(_four[:, None], (NF, 128)).astype(np.float32)


def quartets():
    for d in range(QUAD):
        yield (d, 17 - d, 18 + d, 35 - d)


def iota(shape, dim):
    return lax.broadcasted_iota(jnp.int32, shape, dim)


def pack_edges(ref, g, lane):
    pair = lane // 2
    packed = [jnp.zeros((8, 128), F32) for _ in range(4)]
    for i in range(FG):
        for d in range(HALF):
            h, j = place(i, d)
            here = pair == j // 2
            e = ref[g * GB + i * ND + d]
            packed[h] = jnp.where(here, pltpu.roll(e, (j + 2) % 128, 1), packed[h])
            e = ref[g * GB + i * ND + HALF + d]
            packed[2 + h] = jnp.where(here, pltpu.roll(e, j, 1) if j else e, packed[2 + h])
    return packed


def first_kernel(uneven, spec_hbm, near_w, near_e, send_a, send_b, north, south, msq, spec, sems):
    lane = iota((8, 128), 1)

    def copy(g):
        at = pl.ds(g * GB, GB)
        return pltpu.make_async_copy(spec_hbm.at[at], spec.at[at], sems.at[g])

    for g in range(GROUPS):
        copy(g).start()
    msq[...] = jnp.zeros_like(msq)

    def group(g, growth):
        copy(g).wait()
        total = jnp.zeros((8, 128), F32)
        for i in range(FG):
            acc = jnp.zeros((8, 128), F32)
            for d in range(ND):
                e = spec[g * GB + i * ND + d]
                acc = acc + e
                if d in WESTWARD:
                    k = pl.ds(g * FG * HALF + i * HALF + WESTWARD.index(d), 1)
                    near_w[k, :] = e[0:1]
                else:
                    k = pl.ds(g * FG * HALF + i * HALF + EASTWARD.index(d), 1)
                    near_e[k, :] = e[7:8]
            total = total + float(_slope[i]) * acc
        msq[...] += growth * total
        north[2 * g], north[2 * g + 1], south[2 * g], south[2 * g + 1] = pack_edges(spec, g, lane)
        return growth * float(_slope[FG] / _slope[0])

    lax.fori_loop(0, GROUPS, group, jnp.float32(1.0))
    q = msq[...]
    for near, x in ((near_w, 0), (near_e, 7)):
        near[ROWS : ROWS + 1, :] = q[x : x + 1]
        near[ROWS + 1 : COL, :] = jnp.zeros((COL - ROWS - 1, 128), F32)
    east, west = near_e[...], near_w[...]
    send_a[...] = jnp.where(uneven[0] == 1, west, east)
    send_b[...] = jnp.where(uneven[0] == 1, east, west)


def sector_kernel(mask, winds, wrow, mine):
    for c in range(2):
        for r in range(16):
            mine[0, 16 * c + r : 16 * c + r + 1, :] = winds[c : c + 1, 128 * r : 128 * r + 128]
    mine[0, 32:40, :] = wrow[...].astype(F32)
    mine[0, 40:48, :] = mask[...].astype(F32)
    mine[0, 48:56, :] = jnp.zeros((8, 128), F32)
    rows = mine[0]
    for n in range(1, mine.shape[0]):
        mine[n] = rows


SMEM = pl.BlockSpec(memory_space=pltpu.SMEM)
VMEM = pl.BlockSpec(memory_space=pltpu.VMEM)
HBM = pl.BlockSpec(memory_space=pltpu.HBM)
TILE = jax.ShapeDtypeStruct((8, 128), F32)
FIELD = jax.ShapeDtypeStruct((NF * ND, 8, 128), F32)
STAGE = jax.ShapeDtypeStruct((4 * NF * ND, 8, 128), F32)
BUFFER = pltpu.VMEM((NF * ND, 8, 128), F32)
PARAMS = pltpu.CompilerParams(vmem_limit_bytes=30 * 2**20)
MIDDLE = pltpu.CompilerParams(vmem_limit_bytes=43 * 2**20)
WIDE = pltpu.CompilerParams(vmem_limit_bytes=48 * 2**20)
ALONE = pltpu.CompilerParams(vmem_limit_bytes=54 * 2**20)


def first_call(uneven, spectra):
    edge = jax.ShapeDtypeStruct((COL, 128), F32)
    pack = jax.ShapeDtypeStruct((TILES, 8, 128), F32)
    return pl.pallas_call(
        first_kernel,
        in_specs=[SMEM, HBM],
        out_specs=[VMEM] * 7,
        out_shape=[edge, edge, edge, edge, pack, pack, TILE],
        scratch_shapes=[BUFFER, pltpu.SemaphoreType.DMA((GROUPS,))],
        compiler_params=WIDE,
        name="first",
    )(uneven, spectra)


def sector_call(mask, winds, wrow, lons):
    return pl.pallas_call(
        sector_kernel,
        in_specs=[VMEM] * 3,
        out_specs=VMEM,
        out_shape=jax.ShapeDtypeStruct((lons, 56, 128), F32),
        compiler_params=ALONE,
        name="sector",
    )(mask, winds, wrow)


def split2(x):
    a = x.astype(BF16)
    return a, (x - a.astype(F32)).astype(BF16)


def wind_kernel(
    me_ref, table, wrow, msq, mask, north, south, lane_tab,
    u_ref, v_ref, side_ref, fn, fs,
):
    srcs = table.shape[0]
    me = me_ref[0]
    hi_count = srcs * 16
    west = table.at[(me + srcs - 1) & (srcs - 1)]
    east = table.at[(me + 1) & (srcs - 1)]
    rows = [wrow[x : x + 1, :] for x in range(8)]
    for ref, x in ((west, 7), (east, 0)):
        rows.append(ref[32 + x : 33 + x, :].astype(jnp.int32))
    local = [r & (hi_count * 128 - 1) for r in rows]
    hi_iota = iota((hi_count, 128), 0)
    hots = []
    for r in local:
        hots.append(jnp.where(hi_iota == r // 128, 1.0, 0.0).astype(BF16))
    hot = jnp.concatenate(hots, axis=1)
    tab = jnp.concatenate(
        [table[:, 16 * c : 16 * c + 16].reshape(hi_count, 128) for c in range(2)], axis=1
    )
    got = None
    for part in split2(tab):
        term = lax.dot_general(
            part, hot, (((0,), (0,)), ((), ())), preferred_element_type=F32
        )
        got = term if got is None else got + term
    lo_iota = iota((128, 128), 0)
    us, vs = [], []
    for n, r in enumerate(local):
        pick = lo_iota == (r & 127)
        at = slice(n * 128, n * 128 + 128)
        us.append(jnp.sum(jnp.where(pick, got[0:128, at], 0.0), axis=0, keepdims=True))
        vs.append(jnp.sum(jnp.where(pick, got[128:256, at], 0.0), axis=0, keepdims=True))
    for x in range(8):
        u_ref[x : x + 1, :] = us[x]
        v_ref[x : x + 1, :] = vs[x]
    for n, (ref, x) in enumerate(((west, 7), (east, 0))):
        side_ref[3 * n : 3 * n + 1, :] = us[8 + n]
        side_ref[3 * n + 1 : 3 * n + 2, :] = vs[8 + n]
        side_ref[3 * n + 2 : 3 * n + 3, :] = ref[40 + x : 41 + x, :]
    side_ref[6:8, :] = jnp.zeros((2, 128), F32)

    maskf = mask[...].astype(F32)
    odd = (iota((8, 128), 1) & 1) == 1
    for edge, out, at, sign in ((north, fn, 126, 1.0), (south, fs, 0, -1.0)):
        pick = lambda a: jnp.where(
            odd,
            jnp.broadcast_to(a[:, at + 1 : at + 2], (8, 128)),
            jnp.broadcast_to(a[:, at : at + 1], (8, 128)),
        )
        ue, ve, me_, qe = pick(u_ref[...]), pick(v_ref[...]), pick(maskf), pick(msq[...])
        for n in range(TILES):
            lt = lane_tab[n]
            along = sign * (lt[2:3] * ue + lt[3:4] * ve)
            t = jnp.maximum(lt[0:1] * along + lt[1:2], 1.0)
            out[n * 8 : n * 8 + 8, :] = edge[n] * t * (me_ / (1.0 + lt[4:5] * qe))


def wind_call(me, table, wrow, msq, mask, north, south):
    edge = jax.ShapeDtypeStruct((TILES * 8, 128), F32)
    return pl.pallas_call(
        wind_kernel,
        in_specs=[SMEM] + [VMEM] * 7,
        out_specs=[VMEM] * 5,
        out_shape=[TILE, TILE, TILE, edge, edge],
        compiler_params=PARAMS,
        name="winds",
    )(me, table, wrow, msq, mask, north, south, jnp.asarray(LANE_TAB))


def bin_lane(s, i, row, up):
    north = 2 * (row + (0 if s == 0 else QUAD)) + 1
    south = 2 * (row + (0 if s == 0 else -QUAD))
    return jnp.where(up, north, south) + (i % 3) * ND


def wind_factor(sm, f, along):
    return jnp.maximum(scal(sm, 0, f) * along + scal(sm, 1, f), 1.0)


def put_row(dst_w, dst_e, f, d, e, x_east, x_west):
    if d in WESTWARD:
        dst_w[pl.ds(f * HALF + WESTWARD.index(d), 1), :] = e[x_west : x_west + 1]
    else:
        dst_e[pl.ds(f * HALF + EASTWARD.index(d), 1), :] = e[x_east : x_east + 1]


def along_table(along, u, v):
    for d in range(ND):
        along[d] = float(_cos[d]) * u + float(_sin[d]) * v


def shifted(gv, d):
    return pltpu.roll(gv, 7 if d in WESTWARD else 1, 0), pltpu.roll(gv, 1 if d < HALF else 127, 1)


def lane_patch(tiles_n, tiles_s, i, d, lane):
    h, j = place(i, d % HALF)
    tile, at = (tiles_n[h], 0) if d < HALF else (tiles_s[h], 127)
    return jnp.where(lane == at, pltpu.roll(tile, 127 - j, 1), 0.0)


def group_tiles(ref, g):
    return [ref[pl.ds(pl.multiple_of(g * 16 + 8 * h, 8), 8), :] for h in range(2)]


def step_one_kernel(
    sm, spec_hbm, u, v, msq, mask, out, msq2, in_w, in_e, to_w, to_e, spec, along, sems
):
    def copy(g):
        at = pl.ds(g * GB, GB)
        return pltpu.make_async_copy(spec_hbm.at[at], spec.at[at], sems.at[g])

    for g in range(GROUPS):
        copy(g).start()
    maskf = mask[...].astype(F32)
    along_table(along, u[...], v[...])
    msq2[...] = jnp.zeros_like(msq2)
    for col in (in_w, in_e, to_w, to_e):
        col[ROWS:COL, :] = jnp.zeros((COL - ROWS, 128), F32)

    @pl.loop(0, GROUPS)
    def _(g):
        copy(g).wait()
        total = jnp.zeros((8, 128), F32)
        for i in range(FG):
            f = g * FG + i
            cr = scal(sm, 2, f)
            fac = maskf / (1.0 + scal(sm, 4, f) * msq[...])
            a = scal(sm, 0, f) * fac
            b = scal(sm, 1, f) * fac
            acc = jnp.zeros((8, 128), F32)
            for quartet in quartets():
                d0 = quartet[0]
                kx = cr * float(abs(_cos[d0]))
                ky = cr * float(abs(_sin[d0]))
                k0 = 1.0 - kx - ky
                for d in quartet:
                    gv = spec[f * ND + d] * jnp.maximum(a * along[d] + b, fac)
                    xs, ys = shifted(gv, d)
                    e = k0 * gv + kx * xs + ky * ys
                    out[f * ND + d] = e
                    acc = acc + e
                    put_row(to_w, to_e, f, d, e, 7, 0)
                    put_row(in_e, in_w, f, d, e, 0, 7)
            total = total + scal(sm, 3, f) * acc
        msq2[...] += total


def step_one_call(spectra, u, v, msq, mask):
    column = jax.ShapeDtypeStruct((COL, 128), F32)
    return pl.pallas_call(
        step_one_kernel,
        in_specs=[SMEM, HBM] + [VMEM] * 4,
        out_specs=[VMEM] * 6,
        out_shape=[FIELD, TILE, column, column, column, column],
        scratch_shapes=[
            BUFFER,
            pltpu.VMEM((ND, 8, 128), F32),
            pltpu.SemaphoreType.DMA((GROUPS,)),
        ],
        compiler_params=MIDDLE,
        name="step_one",
    )(jnp.asarray(SCAL), spectra, u, v, msq, mask)


def mend_one_kernel(
    sm, near_w, near_e, own_w, own_e, in_w, in_e, to_w, to_e, part, msq, u, v, mask, side, fn, fs,
    rn, rs, lane_tab, dir_tab, four,
    msq2, row_w, row_e, col_w, col_e, fn2, fs2, patch_n, patch_s, corner,
):
    row18 = iota((HALF, 128), 0)
    lane18 = iota((HALF, 128), 1)
    up = row18 < QUAD
    maskf = mask[...].astype(F32)
    msq2[...] = part[...]
    acc = {}
    for s, (near, own, src, dst, x, far) in enumerate(
        ((near_w, own_e, in_w, row_w, 0, 7), (near_e, own_w, in_e, row_e, 7, 0))
    ):
        cos = dir_tab[2 * s]
        sin = dir_tab[2 * s + 1]
        acos = jnp.abs(cos)
        u_row, v_row, mask_row = (side[3 * s + r : 3 * s + r + 1, :] for r in range(3))
        along = cos * u_row + sin * v_row
        fac = mask_row / (1.0 + four[...] * near[ROWS : ROWS + 1, :])
        along_own = cos * u[far : far + 1, :] + sin * v[far : far + 1, :]
        fac_own = maskf[far : far + 1] / (1.0 + four[...] * msq[far : far + 1, :])
        steep = jnp.zeros((HALF, 128), F32)
        for f in range(NF):
            at = slice(f * HALF, f * HALF + HALF)
            g1 = near[at, :] * wind_factor(sm, f, along) * fac[f : f + 1]
            ring = own[at, :] * wind_factor(sm, f, along_own) * fac_own[f : f + 1]
            fix = (scal(sm, 2, f) * acos) * (g1 - ring)
            dst[at, :] = src[at, :] + fix
            steep = steep + scal(sm, 3, f) * fix
            i = f % FG
            tile = 2 * (f // FG) + i // 3
            ends = jnp.where(
                up,
                jnp.broadcast_to(g1[:, 127:128], (HALF, 128)),
                jnp.broadcast_to(g1[:, 0:1], (HALF, 128)),
            )
            ends = jnp.where(lane18 == bin_lane(s, i, row18, up), ends, 0.0)
            acc[tile] = acc[tile] + ends if tile in acc else ends
        dst[ROWS:COL, :] = jnp.zeros((COL - ROWS, 128), F32)
        msq2[x : x + 1, :] = part[x : x + 1, :] + jnp.sum(steep, axis=0, keepdims=True)
    for tile in range(TILES):
        corner[tile : tile + 1, :] = jnp.sum(acc[tile], axis=0, keepdims=True)

    lane = iota((8, 128), 1)
    for own, halo, dst, odd, at in ((fn, rn, patch_n, 1, 0), (fs, rs, patch_s, 0, 127)):
        steep = jnp.zeros((8, 128), F32)
        for n in range(TILES):
            lt = lane_tab[n]
            rows = slice(n * 8, n * 8 + 8)
            fix = lt[5:6] * jnp.abs(lt[3:4]) * (halo[rows, :] - own[rows, :])
            dst[rows, :] = fix
            steep = steep + lt[6:7] * fix
        steep = jnp.sum(jnp.where((lane & 1) == odd, steep, 0.0), axis=1, keepdims=True)
        msq2[...] += jnp.where(lane == at, steep, 0.0)
    msq2[...] = msq2[...] * maskf

    end = lane18 == jnp.where(up, 0, 127)
    for s, (src, dst, x) in enumerate(((to_e, col_e, 7), (to_w, col_w, 0))):
        along = dir_tab[2 * s] * u[x : x + 1, :] + dir_tab[2 * s + 1] * v[x : x + 1, :]
        fac = maskf[x : x + 1] / (1.0 + four[...] * msq2[x : x + 1, :])
        for f in range(NF):
            at = slice(f * HALF, f * HALF + HALF)
            i = f % FG
            row = (2 * (f // FG) + i // 3) * 8 + x
            fix = jnp.where(up, patch_n[row : row + 1, :], patch_s[row : row + 1, :])
            fix = jnp.where(lane18 == bin_lane(s, i, row18, up), fix, 0.0)
            e = src[at, :] + jnp.where(end, jnp.sum(fix, axis=1, keepdims=True), 0.0)
            dst[at, :] = e * wind_factor(sm, f, along) * fac[f : f + 1]
        dst[ROWS:COL, :] = jnp.zeros((COL - ROWS, 128), F32)

    sub = iota((8, 128), 0)
    for own, dst, at, sign in ((fn, fn2, 127, 1.0), (fs, fs2, 0, -1.0)):
        pick = lambda z: jnp.broadcast_to(z[:, at : at + 1], (8, 128))
        ue, ve, me, qe = pick(u[...]), pick(v[...]), pick(maskf), pick(msq2[...])
        for n in range(TILES):
            lt = lane_tab[n]
            cos, sin = sign * lt[2:3], sign * lt[3:4]
            kx = lt[5:6] * jnp.abs(cos)
            ky = lt[5:6] * jnp.abs(sin)
            g1 = own[n * 8 : n * 8 + 8, :]
            row = corner[n : n + 1, :]
            from_w = jnp.where(sub == 0, row, pltpu.roll(g1, 1, 0))
            from_e = jnp.where(sub == 7, row, pltpu.roll(g1, 7, 0))
            xs = jnp.where(cos > 0.0, from_w, from_e)
            ys = pltpu.roll(g1, 1 if at else 127, 1)
            e = (1.0 - kx - ky) * g1 + kx * xs + ky * ys
            t = jnp.maximum(lt[0:1] * (cos * ue + sin * ve) + lt[1:2], 1.0)
            dst[n * 8 : n * 8 + 8, :] = e * t * (me / (1.0 + lt[4:5] * qe))


def mend_one_call(near_w, near_e, own_w, own_e, in_w, in_e, to_w, to_e, part, msq, u, v, mask, side, fn, fs, rn, rs):
    edge = jax.ShapeDtypeStruct((TILES * 8, 128), F32)
    column = jax.ShapeDtypeStruct((COL, 128), F32)
    return pl.pallas_call(
        mend_one_kernel,
        in_specs=[SMEM] + [VMEM] * 21,
        out_specs=[VMEM] * 9,
        out_shape=[TILE, column, column, column, column, edge, edge, edge, edge],
        scratch_shapes=[pltpu.VMEM((24, 128), F32)],
        compiler_params=PARAMS,
        name="mend_one",
    )(
        jnp.asarray(SCAL), near_w, near_e, own_w, own_e, in_w, in_e, to_w, to_e, part, msq, u, v,
        mask, side, fn, fs, rn, rs, jnp.asarray(LANE_TAB), jnp.asarray(DIR_TAB), jnp.asarray(FOUR_COL),
    )


def step_two_kernel(
    sm, spec, row_w, row_e, u, v, msq, mask, patch_n, patch_s, out, push, out_w, out_e, along, field, sems
):
    def copy(g):
        at = pl.ds(g * GB, GB)
        return pltpu.make_async_copy(field.at[at], out.at[at], sems.at[g])

    lane = iota((8, 128), 1)
    sub = iota((8, 128), 0)
    maskf = mask[...].astype(F32)
    along_table(along, u[...], v[...])
    push[...] = jnp.zeros_like(push)

    @pl.loop(0, GROUPS)
    def _(g):
        pu = jnp.zeros((8, 128), F32)
        pv = jnp.zeros((8, 128), F32)
        tiles_n = group_tiles(patch_n, g)
        tiles_s = group_tiles(patch_s, g)
        for i in range(FG):
            f = g * FG + i
            a, b, cr = scal(sm, 0, f), scal(sm, 1, f), scal(sm, 2, f)
            fac = maskf / (1.0 + scal(sm, 4, f) * msq[...])
            fu = jnp.zeros((8, 128), F32)
            fv = jnp.zeros((8, 128), F32)
            for quartet in quartets():
                d0 = quartet[0]
                kx = cr * float(abs(_cos[d0]))
                ky = cr * float(abs(_sin[d0]))
                k0 = 1.0 - kx - ky
                kxm = kx * maskf
                kym = ky * maskf
                q = []
                for d in quartet:
                    t = jnp.maximum(a * along[d] + b, 1.0)
                    e = spec[f * ND + d]
                    if d in WESTWARD:
                        row = row_e[pl.ds(f * HALF + WESTWARD.index(d), 1), :]
                        e = jnp.where(sub == 7, jnp.broadcast_to(row, (8, 128)), e)
                    else:
                        row = row_w[pl.ds(f * HALF + EASTWARD.index(d), 1), :]
                        e = jnp.where(sub == 0, jnp.broadcast_to(row, (8, 128)), e)
                    e = e + lane_patch(tiles_n, tiles_s, i, d, lane)
                    gv = e * t * fac
                    xs, ys = shifted(gv, d)
                    e = k0 * gv + kxm * xs + kym * ys
                    field[f * ND + d] = e
                    put_row(out_e, out_w, f, d, e, 0, 7)
                    q.append((t - 1.0) * e)
                lo = q[0] - q[2]
                hi = q[1] - q[3]
                fu = fu + float(_cos[d0]) * (lo - hi)
                fv = fv + float(_sin[d0]) * (lo + hi)
            pu = pu + scal(sm, 5, f) * fu
            pv = pv + scal(sm, 5, f) * fv
        push[0] += pu
        push[1] += pv
        copy(g).start()

    for col in (out_w, out_e):
        col[ROWS:COL, :] = jnp.zeros((COL - ROWS, 128), F32)
    for g in range(GROUPS):
        copy(g).wait()


def step_two_call(spec, row_w, row_e, u, v, msq, mask, patch_n, patch_s):
    column = jax.ShapeDtypeStruct((COL, 128), F32)
    return pl.pallas_call(
        step_two_kernel,
        in_specs=[SMEM] + [VMEM] * 9,
        out_specs=[HBM] + [VMEM] * 3,
        out_shape=[STAGE, jax.ShapeDtypeStruct((2, 8, 128), F32), column, column],
        scratch_shapes=[
            pltpu.VMEM((ND, 8, 128), F32),
            BUFFER,
            pltpu.SemaphoreType.DMA((GROUPS,)),
        ],
        compiler_params=PARAMS,
        name="step_two",
    )(jnp.asarray(SCAL), spec, row_w, row_e, u, v, msq, mask, patch_n, patch_s)


def mend_two_kernel(
    sm, halo_w, halo_e, sent_w, sent_e, out_w, out_e, push_in, u, v, mask, owner, weight,
    own_n, own_s, rn, rs, lane_tab, dir_tab,
    end_w, end_e, cells, patch_n, patch_s, push,
):
    maskf = mask[...].astype(F32)
    push[...] = push_in[...]
    for s, (halo, ring, src, dst, x) in enumerate(
        ((halo_w, sent_e, out_w, end_w, 0), (halo_e, sent_w, out_e, end_e, 7))
    ):
        cos = dir_tab[2 * s]
        sin = dir_tab[2 * s + 1]
        along = cos * u[x : x + 1, :] + sin * v[x : x + 1, :]
        weigh = jnp.abs(cos) * maskf[x : x + 1]
        total = jnp.zeros((HALF, 128), F32)
        for f in range(NF):
            at = slice(f * HALF, f * HALF + HALF)
            fix = (scal(sm, 2, f) * weigh) * (halo[at, :] - ring[at, :])
            dst[at, :] = src[at, :] + fix
            total = total + (scal(sm, 5, f) * (wind_factor(sm, f, along) - 1.0)) * fix
        dst[ROWS:COL, :] = jnp.zeros((COL - ROWS, 128), F32)
        for c, part in ((0, cos), (1, sin)):
            push[c, x : x + 1, :] = push_in[c, x : x + 1, :] + jnp.sum(part * total, axis=0, keepdims=True)
    lane = iota((8, 128), 1)
    for own, halo, dst, odd, at, sign in (
        (own_n, rn, patch_n, 1, 0, 1.0), (own_s, rs, patch_s, 0, 127, -1.0)
    ):
        pick = lambda z: jnp.broadcast_to(z[:, at : at + 1], (8, 128))
        ue, ve, me = pick(u[...]), pick(v[...]), pick(maskf)
        tu = jnp.zeros((8, 128), F32)
        tv = jnp.zeros((8, 128), F32)
        for n in range(TILES):
            lt = lane_tab[n]
            rows = slice(n * 8, n * 8 + 8)
            cos, sin = sign * lt[2:3], sign * lt[3:4]
            fix = lt[5:6] * jnp.abs(sin) * me * (halo[rows, :] - own[rows, :])
            dst[rows, :] = fix
            rate = jnp.maximum(lt[0:1] * (cos * ue + sin * ve) + lt[1:2], 1.0) - 1.0
            q = lt[7:8] * rate * fix
            tu = tu + cos * q
            tv = tv + sin * q
        for c, part in ((0, tu), (1, tv)):
            part = jnp.sum(jnp.where((lane & 1) == odd, part, 0.0), axis=1, keepdims=True)
            push[c] += jnp.where(lane == at, part, 0.0)

    uu, vv = u[...], v[...]
    share = weight[...].astype(F32) * maskf
    tau = 0.02 * (uu * uu + vv * vv) + 0.25
    terms = (share, share * tau, share * push[0], share * push[1])
    parts = [split2(t) for t in terms]
    dests = cells.shape[0]
    own = owner[...] & (dests * 512 - 1)
    hi_own = own // 128
    lo_own = own & 127
    row = iota((dests * 16, 128), 0)
    want = (row // 16) * 4 + row % 4
    lo_iota = iota((128, 128), 0)
    kind = iota((16, 128), 0) // 4
    total = jnp.zeros((dests * 16, 128), F32)
    for x in range(8):
        hot = jnp.where(lo_iota == lo_own[x : x + 1], 1.0, 0.0).astype(BF16)
        match = want == hi_own[x : x + 1]
        for p in range(2):
            rows = [parts[k][p][x : x + 1].astype(F32) for k in range(4)]
            tile = jnp.where(
                kind == 0, rows[0],
                jnp.where(kind == 1, rows[1], jnp.where(kind == 2, rows[2], rows[3])),
            )
            lhs = jnp.where(match, jnp.concatenate([tile] * dests, axis=0), 0.0).astype(BF16)
            total = total + lax.dot_general(
                lhs, hot, (((1,), (1,)), ((), ())), preferred_element_type=F32
            )
    cells[...] = total.reshape(dests, 16, 128)


def mend_two_call(
    halo_w, halo_e, sent_w, sent_e, out_w, out_e, push, u, v, mask, owner, weight,
    own_n, own_s, rn, rs, dests,
):
    edge = jax.ShapeDtypeStruct((TILES * 8, 128), F32)
    column = jax.ShapeDtypeStruct((COL, 128), F32)
    return pl.pallas_call(
        mend_two_kernel,
        in_specs=[SMEM] + [VMEM] * 18,
        out_specs=[VMEM] * 5,
        out_shape=[column, column, jax.ShapeDtypeStruct((dests, 16, 128), F32), edge, edge],
        scratch_shapes=[pltpu.VMEM((2, 8, 128), F32)],
        compiler_params=PARAMS,
        name="mend_two",
    )(
        jnp.asarray(SCAL), halo_w, halo_e, sent_w, sent_e, out_w, out_e, push, u, v, mask, owner,
        weight, own_n, own_s, rn, rs, jnp.asarray(LANE_TAB), jnp.asarray(DIR_TAB),
    )


def output_kernel(stage, end_w, end_e, patch_n, patch_s, out, field, whole, sems_in, sems):
    sub = iota((8, 128), 0)
    lane = iota((8, 128), 1)

    def copy_in(g):
        at = pl.ds(g * GB, GB)
        return pltpu.make_async_copy(stage.at[at], field.at[at], sems_in.at[g])

    def copy(g):
        at = pl.ds(g * GB, GB)
        return pltpu.make_async_copy(whole.at[at], out.at[at], sems.at[g])

    for g in range(GROUPS):
        copy_in(g).start()

    @pl.loop(0, GROUPS)
    def _(g):
        copy_in(g).wait()
        tiles_n = group_tiles(patch_n, g)
        tiles_s = group_tiles(patch_s, g)
        for i in range(FG):
            f = g * FG + i
            for d in range(ND):
                if d in WESTWARD:
                    row = end_e[pl.ds(f * HALF + WESTWARD.index(d), 1), :]
                    x = 7
                else:
                    row = end_w[pl.ds(f * HALF + EASTWARD.index(d), 1), :]
                    x = 0
                e = jnp.where(sub == x, jnp.broadcast_to(row, (8, 128)), field[f * ND + d])
                whole[f * ND + d] = e + lane_patch(tiles_n, tiles_s, i, d, lane)
        copy(g).start()

    for g in range(GROUPS):
        copy(g).wait()


def output_call(field, end_w, end_e, patch_n, patch_s):
    return pl.pallas_call(
        output_kernel,
        in_specs=[HBM] + [VMEM] * 4,
        out_specs=HBM,
        out_shape=FIELD,
        scratch_shapes=[
            BUFFER,
            BUFFER,
            pltpu.SemaphoreType.DMA((GROUPS,)),
            pltpu.SemaphoreType.DMA((GROUPS,)),
        ],
        compiler_params=PARAMS,
        name="output",
    )(field, end_w, end_e, patch_n, patch_s)


def cell_kernel(parts, stress, rough):
    sums = jnp.sum(parts[...], axis=0)
    w, a, bx, by = (sums[4 * k : 4 * k + 4] for k in range(4))
    total_w = jnp.maximum(w, 1.0)
    sx = bx / total_w
    sy = by / total_w
    low = jnp.maximum(a, 1.0)
    r = jnp.sqrt(1.0 + (bx * bx + by * by) / (low * low)) * a / total_w
    for n in range(4):
        at = slice(n * 128, n * 128 + 128)
        stress[0:1, at] = sx[n : n + 1]
        stress[1:2, at] = sy[n : n + 1]
        rough[0:1, at] = r[n : n + 1]


def cell_call(parts):
    return pl.pallas_call(
        cell_kernel,
        out_shape=[jax.ShapeDtypeStruct((2, 512), F32), jax.ShapeDtypeStruct((1, 512), F32)],
        compiler_params=ALONE,
        name="cells",
    )(parts)


def body(spectra, sea_mask, atm_wind, wind_row, owner, weight):
    lons = lax.axis_size("lon")
    lats = lax.axis_size("lat")
    me = lax.axis_index("lon").astype(jnp.int32)
    odd = (lax.axis_index("lat") & 1) == 1
    uneven = (lax.axis_index("lon") & 1) == 1
    pairs = [(i, i ^ 1) for i in range(lons)]
    others = [(i, (i + 1 if i & 1 else i - 1) % lons) for i in range(lons)]

    def arrive(send_a, send_b):
        second = lax.ppermute(send_b, "lon", others)
        first = lax.ppermute(send_a, "lon", pairs)
        return jnp.where(uneven, first, second), jnp.where(uneven, second, first)

    def trade(east, west):
        return arrive(jnp.where(uneven, west, east), jnp.where(uneven, east, west))

    inside = [(i, i ^ 1) for i in range(lats)]
    across = [(i, i + 1 if i & 1 else i - 1) for i in range(1, lats - 1)]

    def swap(north, south):
        second = lax.ppermute(jnp.where(odd, north, south), "lat", across)
        first = lax.ppermute(jnp.where(odd, south, north), "lat", inside)
        return jnp.where(odd, first, second), jnp.where(odd, second, first)

    mine = sector_call(sea_mask, atm_wind, wind_row, lons)
    spectra, mine = lax.optimization_barrier((spectra, mine))
    own_w, own_e, send_a, send_b, north, south, msq1 = first_call((me & 1).reshape(1), spectra)
    table = lax.all_to_all(mine, "lon", 0, 0)
    near_w, near_e = arrive(send_a, send_b)
    u, v, side, fn, fs = wind_call(
        me.reshape(1), table, wind_row, msq1, sea_mask, north, south
    )
    rn, rs = swap(fn, fs)
    energy, part, in_w, in_e, to_w, to_e = step_one_call(
        spectra, u, v, msq1, sea_mask
    )
    msq2, row_w, row_e, col_w, col_e, fn2, fs2, patch_n, patch_s = mend_one_call(
        near_w, near_e, own_w, own_e, in_w, in_e, to_w, to_e, part, msq1, u, v, sea_mask, side,
        fn, fs, rn, rs,
    )
    halo_w, halo_e = trade(col_e, col_w)
    rn, rs = swap(fn2, fs2)
    field, push, out_w, out_e = step_two_call(
        energy, row_w, row_e, u, v, msq2, sea_mask, patch_n, patch_s
    )
    end_w, end_e, cells, patch_n, patch_s = mend_two_call(
        halo_w, halo_e, col_w, col_e, out_w, out_e, push, u, v, sea_mask, owner, weight,
        fn2, fs2, rn, rs, lons,
    )
    parts = lax.all_to_all(cells, "lon", 0, 0)
    energy = output_call(field, end_w, end_e, patch_n, patch_s)
    stress, rough = cell_call(parts)
    return energy, stress, rough.reshape(512)


def solution(mesh):
    in_specs = (
        P(None, "lon", "lat"),
        P("lon", "lat"),
        P(None, ("lat", "lon")),
        P("lon", "lat"),
        P("lon", "lat"),
        P("lon", "lat"),
    )
    out_specs = (P(None, "lon", "lat"), P(None, ("lat", "lon")), P(("lat", "lon")))
    return jax.shard_map(body, mesh=mesh, in_specs=in_specs, out_specs=out_specs, check_vma=False)
```
